512 devices in a mesh: tm: 32 (over x, y_hi, core), row: 16 (over z, y_lo).
Axes of the slice: x: 4, y: 8 (y_hi: 4, y_lo: 2; y = y_hi * 2 + y_lo), z: 8, core: 2. Of those that a mesh axis runs over, the one named last changes fastest.
Arguments:
- features: bfloat16 [64, 120, 4096], P('tm', None, 'row'), may hold values from -6 to 6
- self_qkv: bfloat16 [120, 360], replicated, may hold values from -3 to 3
- mutual_qkv: bfloat16 [120, 360], replicated, may hold values from -3 to 3
- out_proj: bfloat16 [240, 120], replicated, may hold values from -1.5 to 1.5
Outputs:
- result: bfloat16 [64, 120, 4096], P('tm', None, 'row')
The draws below stay inside these ranges and needn't reach their ends.
All inputs are finite; a program needn't handle non-finite values.
Results may differ from the reference program's by a relative error of at most 0.0065.
The reference program's roundings to bfloat16 on the way count: a program that leaves them out, or rounds other values in their place, can miss the bound.
Values may be sent and summed in bfloat16 or wider, within the bound.
No kernel may reach another device: no remote copies, remote signals or barrier semaphores. Data moves between devices by JAX's collectives and lax.ppermute only.
A program may use at most 64 MiB of HBM per device.

```python
import jax
import jax.numpy as jnp
from jax import lax

C = 120
HEADS = 6
HD = 20
WIN = 8
CLIP = 2
COLS = 32
FRAMES = 64
H = 128


def draw_features(key, part):
    key = jax.random.fold_in(key, 1)
    noise = jax.random.normal(key, (FRAMES, C, H * COLS), jnp.float32)
    values = noise
    return jnp.clip(values, -6.0, 6.0).astype(jnp.bfloat16)


def draw_self_qkv(key, part):
    key = jax.random.fold_in(key, 2)
    weights = jnp.clip(jax.random.normal(key, (C, 3 * C), jnp.float32), -4.0, 4.0) * C ** (-0.5)
    return weights.astype(jnp.bfloat16)


def draw_mutual_qkv(key, part):
    key = jax.random.fold_in(key, 3)
    weights = jnp.clip(jax.random.normal(key, (C, 3 * C), jnp.float32), -4.0, 4.0) * C ** (-0.5)
    return weights.astype(jnp.bfloat16)


def gaussian(rng, dims, deviation, bound, held_as=jnp.bfloat16):
    values = deviation * jax.random.normal(rng, dims, jnp.float32)
    return jnp.clip(values, min=-bound, max=bound).astype(held_as)


def setup_inputs(seed: int = 0) -> dict:
    arg_keys = jax.random.split(jax.random.key(seed), 5)
    return {
        "features": draw_features(jax.random.fold_in(arg_keys[4], 71), 0),
        "self_qkv": draw_self_qkv(jax.random.fold_in(arg_keys[4], 71), 0),
        "mutual_qkv": draw_mutual_qkv(jax.random.fold_in(arg_keys[4], 71), 0),
        "out_proj": gaussian(arg_keys[3], (2 * C, C), (C // 8) ** -0.5, 1.5),
    }


def layer_norm(values):
    values = values.astype(jnp.float32)
    mean = lax.optimization_barrier(jnp.mean(values, axis=-2, keepdims=True))
    centered = values - mean
    spread = lax.optimization_barrier(jnp.mean(centered * centered, axis=-2, keepdims=True))
    return (centered * lax.rsqrt(spread + 1e-05)).astype(jnp.bfloat16)

def project(values, weights, factor):
    result = jnp.einsum('fcp,cd->fdp', values.astype(jnp.float32), weights.astype(jnp.float32))
    return (result * factor).astype(jnp.bfloat16)

def to_windows(array, heads, win, width):
    frames, chans, flat = array.shape
    rows = flat // width
    shaped = array.reshape(frames, chans, rows, width)
    rolled = jnp.roll(shaped, -(win // 2), axis=3)
    split = rolled.reshape(frames, heads, chans // heads, rows, width // win, win)
    moved = jnp.transpose(split, (4, 1, 2, 0, 3, 5))
    return moved.reshape(width // win, heads, chans // heads, frames * rows * win)

def from_windows(windows, frames, rows, win):
    blocks, heads, depth, tokens = windows.shape
    split = windows.reshape(blocks, heads, depth, frames, rows, win)
    moved = jnp.transpose(split, (3, 1, 2, 4, 0, 5)).reshape(frames, heads * depth, rows, blocks * win)
    rolled = jnp.roll(moved, win // 2, axis=3)
    return rolled.reshape(frames, heads * depth, rows * blocks * win)

def attend(query, keys, values, valid):
    scores = jnp.einsum('nhdq,nhdk->nhqk', query.astype(jnp.float32), keys.astype(jnp.float32))
    scores = jnp.where(valid[:, None, None, :], scores, -1e+30)
    top = lax.optimization_barrier(jnp.max(scores, axis=-1, keepdims=True))
    weights = jnp.exp(scores - top)
    weights = (weights / lax.optimization_barrier(jnp.sum(weights, axis=-1, keepdims=True))).astype(jnp.bfloat16)
    out = jnp.einsum('nhqk,nhdk->nhdq', weights.astype(jnp.float32), values.astype(jnp.float32))
    return out.astype(jnp.bfloat16)

def reference(features, self_qkv, mutual_qkv, out_proj):
    frames_all, chans, flat = features.shape
    width = COLS
    height = flat // width
    clips = frames_all // CLIP
    half = WIN // 2
    blocks = width // WIN
    window_rows = height // WIN + 1
    scale = HD ** (-0.5)
    padded = jnp.pad(features, ((CLIP, CLIP), (0, 0), (half * width, half * width)))
    row_ids = jnp.arange(height + 2 * half, dtype=jnp.int32)
    rows_ok = (row_ids >= half) & (row_ids < height + half)

    def one_clip(clip):
        block = lax.dynamic_slice_in_dim(padded, (clip * CLIP).astype(jnp.int32), 3 * CLIP, 0)
        normed = layer_norm(block)
        own = normed[CLIP:2 * CLIP]
        neighbours = jnp.concatenate([normed[:CLIP], normed[2 * CLIP:]], axis=0)
        query_self = project(own, self_qkv[:, :chans], scale)
        kv_self = project(own, self_qkv[:, chans:], 1.0)
        query_mutual = project(own, mutual_qkv[:, :chans], scale)
        kv_mutual = project(neighbours, mutual_qkv[:, chans:], 1.0)
        before_ok = clip > 0
        after_ok = clip < clips - 1

        def one_row(index):
            start = (index * WIN * width).astype(jnp.int32)

            def cut(array):
                return lax.dynamic_slice_in_dim(array, start, WIN * width, 2)
            row_flags = lax.dynamic_slice_in_dim(rows_ok, (index * WIN).astype(jnp.int32), WIN, 0)
            token_flags = jnp.broadcast_to(row_flags[None, :, None], (CLIP, WIN, WIN)).reshape(-1)
            self_flags = jnp.broadcast_to(token_flags[None], (blocks, token_flags.shape[0]))
            mutual_tokens = jnp.concatenate([token_flags & before_ok, token_flags & after_ok])
            mutual_flags = jnp.broadcast_to(mutual_tokens[None], (blocks, mutual_tokens.shape[0]))
            kv_rows = cut(kv_self)
            out_self = attend(to_windows(cut(query_self), HEADS, WIN, width), to_windows(kv_rows[:, :chans], HEADS, WIN, width), to_windows(kv_rows[:, chans:], HEADS, WIN, width), self_flags)
            mutual_rows = cut(kv_mutual)
            out_mutual = attend(to_windows(cut(query_mutual), HEADS, WIN, width), to_windows(mutual_rows[:, :chans], HEADS, WIN, width), to_windows(mutual_rows[:, chans:], HEADS, WIN, width), mutual_flags)
            back_self = from_windows(out_self, CLIP, WIN, WIN)
            back_mutual = from_windows(out_mutual, CLIP, WIN, WIN)
            return jnp.concatenate([back_mutual, back_self], axis=1)
        gathered = lax.map(one_row, jnp.arange(window_rows, dtype=jnp.int32))
        mixed = jnp.transpose(gathered, (1, 2, 0, 3)).reshape(CLIP, 2 * chans, window_rows * WIN * width)
        mixed = mixed[:, :, half * width:half * width + height * width]
        branch = jnp.einsum('fcp,cd->fdp', mixed.astype(jnp.float32), out_proj.astype(jnp.float32))
        start_frame = (clip * CLIP).astype(jnp.int32)
        residual = lax.dynamic_slice_in_dim(features, start_frame, CLIP, 0).astype(jnp.float32)
        return (residual + branch).astype(jnp.bfloat16)
    result = lax.map(one_clip, jnp.arange(clips, dtype=jnp.int32))
    return result.reshape(frames_all, chans, flat)
```

```python
import functools

import jax
import jax.numpy as jnp
from jax import lax
from jax.experimental import pallas as pl
from jax.experimental.pallas import tpu as pltpu
from jax.sharding import PartitionSpec as P

C = 120
HEADS = 6
HD = 20
WIN = 8
COLS = 32
HALF = WIN // 2
TOK = HALF * COLS
GROUPS = COLS // WIN
PART = HALF * WIN
LANES = 128
NEG = -1e30
F32 = jnp.float32
BF16 = jnp.bfloat16

NN = (((1,), (0,)), ((), ()))
NT = (((1,), (1,)), ((), ()))


def iota(shape, dim):
    return lax.broadcasted_iota(jnp.int32, shape, dim)


def dot(a, b, dims=NN):
    return lax.dot_general(a, b, dims, preferred_element_type=F32)


def window_order(transposed=False):
    tok, pos = (1, 0) if transposed else (0, 1)
    t = iota((TOK, TOK), tok)
    p = iota((TOK, TOK), pos)
    column = ((t // PART) * WIN + t % WIN + HALF) % COLS
    row = (t % PART) // WIN
    return jnp.where(row * COLS + column == p, 1.0, 0.0).astype(BF16)


def normalize(x, invalid):
    x = x.astype(F32)
    mean = jnp.mean(x, axis=0, keepdims=True)
    centered = x - mean
    spread = jnp.mean(centered * centered, axis=0, keepdims=True)
    normed = centered * lax.rsqrt(spread + 1e-05)
    sub = iota((LANES - C, x.shape[1]), 0)
    extra = jnp.where(sub == 0, invalid, jnp.where(sub == 1, 1.0, 0.0))
    return jnp.concatenate([normed, extra], axis=0).astype(BF16)


def padded(weights, part, at=None, value=0.0):
    w = weights[:, part * C : (part + 1) * C].astype(F32)
    w = jnp.concatenate([w, jnp.zeros((C, LANES - C), F32)], axis=1)
    w = jnp.concatenate([w, jnp.zeros((LANES - C, LANES), F32)], axis=0)
    if at is not None:
        hit = (iota((LANES, LANES), 0) == at) & (iota((LANES, LANES), 1) == C)
        w = jnp.where(hit, value, w)
    return w.astype(BF16)


def query_weights(weights):
    return padded(weights, 0, C + 1, 1.0)


def kv_weights(weights):
    return jnp.concatenate([padded(weights, 1, C, NEG), padded(weights, 2)], axis=1)


def attend(q, k, v):
    lane = iota((1, LANES), 1)
    head_of = lane // HD
    flag = lane == C
    zero = jnp.zeros_like(q)
    spread = jnp.concatenate(
        [jnp.where((head_of == h) & (lane < C) | flag, q, zero) for h in range(HEADS)], axis=0
    )
    scores = dot(spread, k, NT)
    top = jnp.max(scores, axis=-1, keepdims=True)
    weights = jnp.exp(scores - top)
    weights = weights * (1.0 / jnp.sum(weights, axis=-1, keepdims=True))
    out = dot(weights.astype(BF16), v)
    n = q.shape[0]
    total = jnp.zeros((n, LANES), F32)
    for h in range(HEADS):
        total = jnp.where((head_of == h) & (lane < C), out[h * n : (h + 1) * n], total)
    return total.astype(BF16)


def tokens(pair, order, s):
    both = jnp.concatenate([x[:, s * TOK : (s + 1) * TOK] for x in pair], axis=0)
    out = dot(order, both, NT).astype(BF16)
    return out[:, :LANES], out[:, LANES:]


def row_flags(lanes):
    row = lax.axis_index("row")
    strip = iota((1, lanes), 1) // TOK
    above = (strip == 0) & (row == 0)
    below = (strip == 3) & (row == lax.axis_size("row") - 1)
    return above | below


def store_keys(k_ref, v_ref, kv, group, slot):
    for n in range(GROUPS):
        w = group * GROUPS + n
        part = kv[n * PART : (n + 1) * PART].astype(BF16)
        k_ref[w, slot * PART : (slot + 1) * PART, :] = part[:, :LANES]
        v_ref[w, slot * PART : (slot + 1) * PART, :] = part[:, LANES:]


def windows(q_ref, k_ref, v_ref, out_ref):
    @pl.loop(0, 2)
    def _(g):
        @pl.loop(0, GROUPS)
        def _(n):
            w = g * GROUPS + n
            out = attend(q_ref[w], k_ref[w], v_ref[w])
            start = pl.multiple_of(n * PART, PART)
            for f in range(2):
                out_ref[f, g, pl.ds(start, PART), :] = out[f * PART : (f + 1) * PART]


def self_kernel(block_ref, self_ref, mutual_ref, out_ref, qm_ref, q_ref, k_ref, v_ref):
    invalid = jnp.where(row_flags(4 * TOK), 1.0, 0.0)
    order = window_order()
    pair = [normalize(block_ref[f], invalid) for f in range(2)]
    wkv = kv_weights(self_ref)
    wq = jnp.concatenate([query_weights(self_ref), query_weights(mutual_ref)], axis=1)
    scale = HD ** (-0.5)
    for s in range(4):
        for f, tok in enumerate(tokens(pair, order, s)):
            store_keys(k_ref, v_ref, dot(tok, wkv), s // 2, (s % 2) * 2 + f)
            if s in (1, 2):
                q = (dot(tok, wq) * scale).astype(BF16)
                for n in range(GROUPS):
                    w = (s - 1) * GROUPS + n
                    part = q[n * PART : (n + 1) * PART]
                    q_ref[w, f * PART : (f + 1) * PART, :] = part[:, :LANES]
                    qm_ref[w, f * PART : (f + 1) * PART, :] = part[:, LANES:]
    windows(q_ref, k_ref, v_ref, out_ref)


def mutual_kernel(
    before_ref, after_ref, features_ref, mutual_ref, proj_ref, qm_ref, self_out_ref,
    result_ref, k_ref, v_ref, attn_ref,
):
    clip = lax.axis_index("tm")
    bad_rows = row_flags(4 * TOK)
    order = window_order()
    wkv = kv_weights(mutual_ref)
    for side, ref in enumerate((before_ref, after_ref)):
        edge = clip == (0 if side == 0 else lax.axis_size("tm") - 1)
        invalid = jnp.where(bad_rows | edge, 1.0, 0.0)
        pair = [normalize(ref[f], invalid) for f in range(2)]
        for s in range(4):
            for f, tok in enumerate(tokens(pair, order, s)):
                store_keys(k_ref, v_ref, dot(tok, wkv), s // 2, (s % 2) * 4 + side * 2 + f)
    windows(qm_ref, k_ref, v_ref, attn_ref)
    back = window_order(transposed=True)
    proj = proj_ref[...].astype(F32)
    gap = jnp.zeros((LANES - C, C), F32)
    proj = jnp.concatenate([proj[:C], gap, proj[C:], gap], axis=0).astype(BF16)
    for f in range(2):
        for g in range(2):
            mixed = jnp.concatenate([attn_ref[f, g], self_out_ref[f, g]], axis=1)
            mixed = dot(back, mixed).astype(BF16)
            branch = dot(mixed, proj).T
            cut = slice(g * TOK, (g + 1) * TOK)
            result_ref[f, :, cut] = (features_ref[f, :, cut].astype(F32) + branch).astype(BF16)


def vmem(count):
    return [pl.BlockSpec(memory_space=pltpu.VMEM)] * count


def shift(x, axis, step):
    count = lax.axis_size(axis)
    pairs = [(i, i + step) for i in range(count) if 0 <= i + step < count]
    return lax.ppermute(x, axis, pairs)


def on_device(features, self_qkv, mutual_qkv, out_proj):
    up = shift(features[:, :, TOK:], "row", 1)
    down = shift(features[:, :, :TOK], "row", -1)
    block = jnp.concatenate([up, features, down], axis=2)
    before = shift(block, "tm", 1)
    after = shift(block, "tm", -1)
    nw = 2 * GROUPS
    self_out, qm = pl.pallas_call(
        self_kernel,
        out_shape=[
            jax.ShapeDtypeStruct((2, 2, TOK, LANES), BF16),
            jax.ShapeDtypeStruct((nw, 2 * PART, LANES), BF16),
        ],
        in_specs=vmem(3),
        out_specs=vmem(2),
        scratch_shapes=[
            pltpu.VMEM((nw, 2 * PART, LANES), BF16),
            pltpu.VMEM((nw, 4 * PART, LANES), BF16),
            pltpu.VMEM((nw, 4 * PART, LANES), BF16),
        ],
        compiler_params=pltpu.CompilerParams(vmem_limit_bytes=16 * 1024 * 1024),
        cost_estimate=pl.CostEstimate(
            flops=2 * 10**9, bytes_accessed=10**6, transcendentals=400000
        ),
        name="self_attention",
    )(block, self_qkv, mutual_qkv)
    return pl.pallas_call(
        mutual_kernel,
        out_shape=jax.ShapeDtypeStruct(features.shape, BF16),
        in_specs=vmem(7),
        out_specs=pl.BlockSpec(memory_space=pltpu.VMEM),
        scratch_shapes=[
            pltpu.VMEM((nw, 8 * PART, LANES), BF16),
            pltpu.VMEM((nw, 8 * PART, LANES), BF16),
            pltpu.VMEM((2, 2, TOK, LANES), BF16),
        ],
        compiler_params=pltpu.CompilerParams(vmem_limit_bytes=16 * 1024 * 1024),
        cost_estimate=pl.CostEstimate(
            flops=2 * 10**9, bytes_accessed=10**6, transcendentals=800000
        ),
        name="mutual_attention",
    )(before, after, features, mutual_qkv, out_proj, qm, self_out)


def solution(mesh):
    in_specs = (P("tm", None, "row"), P(), P(), P())
    out_specs = P("tm", None, "row")
    return jax.shard_map(
        on_device, mesh=mesh, in_specs=in_specs, out_specs=out_specs, check_vma=False
    )
```

```python
import functools

import jax
import jax.numpy as jnp
from jax import lax
from jax.experimental import pallas as pl
from jax.experimental.pallas import tpu as pltpu
from jax.sharding import PartitionSpec as P

C = 120
HEADS = 6
HD = 20
WIN = 8
COLS = 32
HALF = WIN // 2
TOK = HALF * COLS
GROUPS = COLS // WIN
PART = HALF * WIN
LANES = 128
NEG = -1e30
F32 = jnp.float32
BF16 = jnp.bfloat16

NN = (((1,), (0,)), ((), ()))
NT = (((1,), (1,)), ((), ()))


def iota(shape, dim):
    return lax.broadcasted_iota(jnp.int32, shape, dim)


def dot(a, b, dims=NN):
    return lax.dot_general(a, b, dims, preferred_element_type=F32)


def window_order(transposed=False):
    tok, pos = (1, 0) if transposed else (0, 1)
    t = iota((TOK, TOK), tok)
    p = iota((TOK, TOK), pos)
    column = ((t // PART) * WIN + t % WIN + HALF) % COLS
    row = (t % PART) // WIN
    return jnp.where(row * COLS + column == p, 1.0, 0.0).astype(BF16)


def normalize(x, invalid):
    x = x.astype(F32)
    mean = jnp.mean(x, axis=0, keepdims=True)
    centered = x - mean
    spread = jnp.mean(centered * centered, axis=0, keepdims=True)
    normed = centered * lax.rsqrt(spread + 1e-05)
    sub = iota((LANES - C, x.shape[1]), 0)
    extra = jnp.where(sub == 0, invalid, jnp.where(sub == 1, 1.0, 0.0))
    return jnp.concatenate([normed, extra], axis=0).astype(BF16)


def padded(weights, part, at=None, value=0.0):
    w = weights[:, part * C : (part + 1) * C].astype(F32)
    w = jnp.concatenate([w, jnp.zeros((C, LANES - C), F32)], axis=1)
    w = jnp.concatenate([w, jnp.zeros((LANES - C, LANES), F32)], axis=0)
    if at is not None:
        hit = (iota((LANES, LANES), 0) == at) & (iota((LANES, LANES), 1) == C)
        w = jnp.where(hit, value, w)
    return w.astype(BF16)


def query_weights(weights):
    return padded(weights, 0, C + 1, 1.0)


def kv_weights(weights):
    return jnp.concatenate([padded(weights, 1, C, NEG), padded(weights, 2)], axis=1)


def attend(q, k, v):
    lane = iota((1, LANES), 1)
    head_of = lane // HD
    flag = lane == C
    zero = jnp.zeros_like(q)
    spread = jnp.concatenate(
        [jnp.where((head_of == h) & (lane < C) | flag, q, zero) for h in range(HEADS)], axis=0
    )
    scores = dot(spread, k, NT)
    top = jnp.max(scores, axis=-1, keepdims=True)
    weights = jnp.exp(scores - top)
    weights = weights * (1.0 / jnp.sum(weights, axis=-1, keepdims=True))
    out = dot(weights.astype(BF16), v)
    n = q.shape[0]
    total = jnp.zeros((n, LANES), F32)
    for h in range(HEADS):
        total = jnp.where((head_of == h) & (lane < C), out[h * n : (h + 1) * n], total)
    return total.astype(BF16)


def tokens(pair, order, s):
    both = jnp.concatenate([x[:, s * TOK : (s + 1) * TOK] for x in pair], axis=0)
    out = dot(order, both, NT).astype(BF16)
    return out[:, :LANES], out[:, LANES:]


def row_flags(lanes):
    row = lax.axis_index("row")
    strip = iota((1, lanes), 1) // TOK
    above = (strip == 0) & (row == 0)
    below = (strip == 3) & (row == lax.axis_size("row") - 1)
    return above | below


def store_keys(k_ref, v_ref, kv, group, slot):
    for n in range(GROUPS):
        w = group * GROUPS + n
        part = kv[n * PART : (n + 1) * PART].astype(BF16)
        k_ref[w, slot * PART : (slot + 1) * PART, :] = part[:, :LANES]
        v_ref[w, slot * PART : (slot + 1) * PART, :] = part[:, LANES:]


def windows(q_ref, k_ref, v_ref, out_ref):
    @pl.loop(0, 2)
    def _(g):
        @pl.loop(0, GROUPS)
        def _(n):
            w = g * GROUPS + n
            out = attend(q_ref[w], k_ref[w], v_ref[w])
            start = pl.multiple_of(n * PART, PART)
            for f in range(2):
                out_ref[f, g, pl.ds(start, PART), :] = out[f * PART : (f + 1) * PART]


def self_kernel(block_ref, self_ref, mutual_ref, out_ref, qm_ref, q_ref, k_ref, v_ref):
    invalid = jnp.where(row_flags(4 * TOK), 1.0, 0.0)
    order = window_order()
    pair = [normalize(block_ref[f], invalid) for f in range(2)]
    wkv = kv_weights(self_ref)
    wq = jnp.concatenate([query_weights(self_ref), query_weights(mutual_ref)], axis=1)
    scale = HD ** (-0.5)
    for s in range(4):
        for f, tok in enumerate(tokens(pair, order, s)):
            store_keys(k_ref, v_ref, dot(tok, wkv), s // 2, (s % 2) * 2 + f)
            if s in (1, 2):
                q = (dot(tok, wq) * scale).astype(BF16)
                for n in range(GROUPS):
                    w = (s - 1) * GROUPS + n
                    part = q[n * PART : (n + 1) * PART]
                    q_ref[w, f * PART : (f + 1) * PART, :] = part[:, :LANES]
                    qm_ref[w, f * PART : (f + 1) * PART, :] = part[:, LANES:]
    windows(q_ref, k_ref, v_ref, out_ref)


def mutual_kernel(
    near_ref, far_ref, features_ref, mutual_ref, proj_ref, qm_ref, self_out_ref,
    result_ref, k_ref, v_ref, attn_ref,
):
    clip = lax.axis_index("tm")
    bad_rows = row_flags(4 * TOK)
    order = window_order()
    wkv = kv_weights(mutual_ref)
    for side, ref in enumerate((near_ref, far_ref)):
        edge = (clip == 0) | (clip == lax.axis_size("tm") - 1)
        invalid = jnp.where(bad_rows | edge if side else bad_rows, 1.0, 0.0)
        pair = [normalize(ref[f], invalid) for f in range(2)]
        for s in range(4):
            for f, tok in enumerate(tokens(pair, order, s)):
                store_keys(k_ref, v_ref, dot(tok, wkv), s // 2, (s % 2) * 4 + side * 2 + f)
    windows(qm_ref, k_ref, v_ref, attn_ref)
    back = window_order(transposed=True)
    proj = proj_ref[...].astype(F32)
    gap = jnp.zeros((LANES - C, C), F32)
    proj = jnp.concatenate([proj[:C], gap, proj[C:], gap], axis=0).astype(BF16)
    for f in range(2):
        for g in range(2):
            mixed = jnp.concatenate([attn_ref[f, g], self_out_ref[f, g]], axis=1)
            mixed = dot(back, mixed).astype(BF16)
            branch = dot(mixed, proj).T
            cut = slice(g * TOK, (g + 1) * TOK)
            result_ref[f, :, cut] = (features_ref[f, :, cut].astype(F32) + branch).astype(BF16)


def vmem(count):
    return [pl.BlockSpec(memory_space=pltpu.VMEM)] * count


def swap(x, axis, first):
    pairs = [(i, i + 1) for i in range(first, lax.axis_size(axis) - 1, 2)]
    return lax.ppermute(x, axis, pairs + [(j, i) for i, j in pairs])


def on_device(features, self_qkv, mutual_qkv, out_proj):
    even = lax.axis_index("row") % 2 == 0
    top, bottom = features[:, :, :TOK], features[:, :, TOK:]
    far = swap(jnp.where(even, top, bottom), "row", 1)
    near = swap(jnp.where(even, bottom, top), "row", 0)
    up = jnp.where(even, far, near)
    down = jnp.where(even, near, far)
    block = jnp.concatenate([up, features, down], axis=2)
    far = swap(block, "tm", 1)
    near = swap(block, "tm", 0)
    nw = 2 * GROUPS
    self_out, qm = pl.pallas_call(
        self_kernel,
        out_shape=[
            jax.ShapeDtypeStruct((2, 2, TOK, LANES), BF16),
            jax.ShapeDtypeStruct((nw, 2 * PART, LANES), BF16),
        ],
        in_specs=vmem(3),
        out_specs=vmem(2),
        scratch_shapes=[
            pltpu.VMEM((nw, 2 * PART, LANES), BF16),
            pltpu.VMEM((nw, 4 * PART, LANES), BF16),
            pltpu.VMEM((nw, 4 * PART, LANES), BF16),
        ],
        compiler_params=pltpu.CompilerParams(vmem_limit_bytes=16 * 1024 * 1024),
        cost_estimate=pl.CostEstimate(
            flops=2 * 10**9, bytes_accessed=10**6, transcendentals=400000
        ),
        name="self_attention",
    )(block, self_qkv, mutual_qkv)
    return pl.pallas_call(
        mutual_kernel,
        out_shape=jax.ShapeDtypeStruct(features.shape, BF16),
        in_specs=vmem(7),
        out_specs=pl.BlockSpec(memory_space=pltpu.VMEM),
        scratch_shapes=[
            pltpu.VMEM((nw, 8 * PART, LANES), BF16),
            pltpu.VMEM((nw, 8 * PART, LANES), BF16),
            pltpu.VMEM((2, 2, TOK, LANES), BF16),
        ],
        compiler_params=pltpu.CompilerParams(vmem_limit_bytes=16 * 1024 * 1024),
        cost_estimate=pl.CostEstimate(
            flops=2 * 10**9, bytes_accessed=10**6, transcendentals=800000
        ),
        name="mutual_attention",
    )(near, far, features, mutual_qkv, out_proj, qm, self_out)


def solution(mesh):
    in_specs = (P("tm", None, "row"), P(), P(), P())
    out_specs = P("tm", None, "row")
    return jax.shard_map(
        on_device, mesh=mesh, in_specs=in_specs, out_specs=out_specs, check_vma=False
    )
```

```python
import jax
import jax.numpy as jnp
from jax import lax
from jax.experimental import pallas as pl
from jax.experimental.pallas import tpu as pltpu
from jax.sharding import PartitionSpec as P

C = 120
HEADS = 6
HD = 20
WIN = 8
COLS = 32
HALF = WIN // 2
TOK = HALF * COLS
GROUPS = COLS // WIN
PART = HALF * WIN
LANES = 128
NEG = -1e30
F32 = jnp.float32
BF16 = jnp.bfloat16

NN = (((1,), (0,)), ((), ()))
NT = (((1,), (1,)), ((), ()))


def iota(shape, dim):
    return lax.broadcasted_iota(jnp.int32, shape, dim)


def dot(a, b, dims=NN):
    return lax.dot_general(a, b, dims, preferred_element_type=F32)


def window_order(transposed=False):
    tok, pos = (1, 0) if transposed else (0, 1)
    t = iota((TOK, TOK), tok)
    p = iota((TOK, TOK), pos)
    column = ((t // PART) * WIN + t % WIN + HALF) % COLS
    row = (t % PART) // WIN
    return jnp.where(row * COLS + column == p, 1.0, 0.0).astype(BF16)


def normalize(x, invalid):
    x = x.astype(F32)
    mean = jnp.mean(x, axis=0, keepdims=True)
    centered = x - mean
    spread = jnp.mean(centered * centered, axis=0, keepdims=True)
    normed = centered * lax.rsqrt(spread + 1e-05)
    sub = iota((LANES - C, x.shape[1]), 0)
    extra = jnp.where(sub == 0, invalid, jnp.where(sub == 1, 1.0, 0.0))
    return jnp.concatenate([normed, extra], axis=0).astype(BF16)


def padded(weights, part, at=None, value=0.0):
    w = weights[:, part * C : (part + 1) * C].astype(F32)
    w = jnp.concatenate([w, jnp.zeros((C, LANES - C), F32)], axis=1)
    w = jnp.concatenate([w, jnp.zeros((LANES - C, LANES), F32)], axis=0)
    if at is not None:
        hit = (iota((LANES, LANES), 0) == at) & (iota((LANES, LANES), 1) == C)
        w = jnp.where(hit, value, w)
    return w.astype(BF16)


def query_weights(weights):
    return padded(weights, 0, C + 1, 1.0)


def kv_weights(weights):
    return jnp.concatenate([padded(weights, 1, C, NEG), padded(weights, 2)], axis=1)


def attend(q, k, v):
    lane = iota((1, LANES), 1)
    head_of = lane // HD
    flag = lane == C
    zero = jnp.zeros_like(q)
    spread = jnp.concatenate(
        [jnp.where((head_of == h) & (lane < C) | flag, q, zero) for h in range(HEADS)], axis=0
    )
    scores = dot(spread, k, NT)
    top = jnp.max(scores, axis=-1, keepdims=True)
    weights = jnp.exp(scores - top)
    weights = weights * (1.0 / jnp.sum(weights, axis=-1, keepdims=True))
    out = dot(weights.astype(BF16), v)
    n = q.shape[0]
    total = jnp.zeros((n, LANES), F32)
    for h in range(HEADS):
        total = jnp.where((head_of == h) & (lane < C), out[h * n : (h + 1) * n], total)
    return total.astype(BF16)


def tokens(pair, order):
    out = dot(order, jnp.concatenate(pair, axis=0), NT).astype(BF16)
    return out[:, :LANES], out[:, LANES:]


def own_kernel(
    features_ref, self_ref, mutual_ref, proj_ref,
    tok_ref, wq_ref, wkv_self_ref, wkv_mutual_ref, proj_out_ref,
):
    order = window_order()
    for s in range(2):
        cut = slice(s * TOK, (s + 1) * TOK)
        pair = [normalize(features_ref[f, :, cut], 0.0) for f in range(2)]
        for f, tok in enumerate(tokens(pair, order)):
            tok_ref[f, s] = tok
    wq_ref[...] = jnp.concatenate([query_weights(self_ref), query_weights(mutual_ref)], axis=1)
    wkv_self_ref[...] = kv_weights(self_ref)
    wkv_mutual_ref[...] = kv_weights(mutual_ref)
    proj = proj_ref[...].astype(F32)
    gap = jnp.zeros((LANES - C, C), F32)
    proj = jnp.concatenate([proj[:C], gap, proj[C:], gap], axis=0)
    proj_out_ref[...] = proj.T.astype(BF16)


def halo_kernel(far_ref, near_ref, own_ref, block_ref):
    order = window_order()
    row = lax.axis_index("row")
    even = lax.rem(row, 2) == 0
    top = jnp.where(row == 0, 1.0, 0.0)
    bottom = jnp.where(row == lax.axis_size("row") - 1, 1.0, 0.0)
    for s, invalid in ((0, top), (3, bottom)):
        pair = []
        for f in range(2):
            far, near = far_ref[f].astype(F32), near_ref[f].astype(F32)
            pair.append(normalize(jnp.where(even == (s == 0), far, near), invalid))
        for f, tok in enumerate(tokens(pair, order)):
            block_ref[f, s] = tok
    for f in range(2):
        for s in range(2):
            block_ref[f, s + 1] = own_ref[f, s]


def store_keys(k_ref, v_ref, kv, group, slot):
    for n in range(GROUPS):
        w = group * GROUPS + n
        part = kv[n * PART : (n + 1) * PART].astype(BF16)
        k_ref[w, slot * PART : (slot + 1) * PART, :] = part[:, :LANES]
        v_ref[w, slot * PART : (slot + 1) * PART, :] = part[:, LANES:]


def store_windows(out_ref, out, g, n):
    for f in range(2):
        out_ref[f, g, n * PART : (n + 1) * PART, :] = out[f * PART : (f + 1) * PART]


def self_kernel(block_ref, wq_ref, wkv_ref, out_ref, qm_ref, q_ref, k_ref, v_ref):
    scale = HD ** (-0.5)
    for s in range(4):
        for f in range(2):
            tok = block_ref[f, s]
            store_keys(k_ref, v_ref, dot(tok, wkv_ref[...]), s // 2, (s % 2) * 2 + f)
            if s in (1, 2):
                q = (dot(tok, wq_ref[...]) * scale).astype(BF16)
                for n in range(GROUPS):
                    w = (s - 1) * GROUPS + n
                    part = q[n * PART : (n + 1) * PART]
                    q_ref[w, f * PART : (f + 1) * PART, :] = part[:, :LANES]
                    qm_ref[w, f * PART : (f + 1) * PART, :] = part[:, LANES:]
    for w in range(2 * GROUPS):
        out = attend(q_ref[w], k_ref[w], v_ref[w])
        store_windows(out_ref, out, w // GROUPS, w % GROUPS)


def near_kernel(near_ref, wkv_ref, k_ref, v_ref):
    for s in range(4):
        for f in range(2):
            kv = dot(near_ref[f, s], wkv_ref[...])
            store_keys(k_ref, v_ref, kv, s // 2, (s % 2) * 2 + f)


def mutual_kernel(
    far_ref, wkv_ref, knear_ref, vnear_ref, qm_ref, self_out_ref, features_ref, proj_ref,
    result_ref, k_ref, v_ref, attn_ref,
):
    clip = lax.axis_index("tm")
    edge = (clip == 0) | (clip == lax.axis_size("tm") - 1)
    flag = jnp.where((iota((1, LANES), 1) == C) & edge, 1.0, 0.0).astype(BF16)
    back = window_order(transposed=True)
    for g in range(2):
        for s in range(2):
            for f in range(2):
                kv = dot(far_ref[f, 2 * g + s] + flag, wkv_ref[...])
                store_keys(k_ref, v_ref, kv, g, s * 2 + f)
    for g in range(2):
        for n in range(GROUPS):
            w = g * GROUPS + n
            k = jnp.concatenate([knear_ref[w], k_ref[w]], axis=0)
            v = jnp.concatenate([vnear_ref[w], v_ref[w]], axis=0)
            store_windows(attn_ref, attend(qm_ref[w], k, v), g, n)
        for f in range(2):
            mixed = jnp.concatenate([attn_ref[f, g], self_out_ref[f, g]], axis=1)
            mixed = dot(back, mixed).astype(BF16)
            branch = dot(proj_ref[...], mixed, NT)
            cut = slice(g * TOK, (g + 1) * TOK)
            result_ref[f, :, cut] = (features_ref[f, :, cut].astype(F32) + branch).astype(BF16)


def call(kernel, outs, args, scratch=(), cost=10**9, name=None):
    return pl.pallas_call(
        kernel,
        out_shape=[jax.ShapeDtypeStruct(shape, BF16) for shape in outs],
        in_specs=[pl.BlockSpec(memory_space=pltpu.VMEM)] * len(args),
        out_specs=[pl.BlockSpec(memory_space=pltpu.VMEM)] * len(outs),
        scratch_shapes=[pltpu.VMEM(shape, BF16) for shape in scratch],
        compiler_params=pltpu.CompilerParams(vmem_limit_bytes=16 * 1024 * 1024),
        cost_estimate=pl.CostEstimate(flops=cost, bytes_accessed=10**6, transcendentals=0),
        name=name,
    )(*args)


def swap(x, axis, first):
    pairs = [(i, i + 1) for i in range(first, lax.axis_size(axis) - 1, 2)]
    return lax.ppermute(x, axis, pairs + [(j, i) for i, j in pairs])


def on_device(features, self_qkv, mutual_qkv, out_proj):
    even = lax.axis_index("row") % 2 == 0
    top, bottom = features[:, :, :TOK], features[:, :, TOK:]
    far_rows = swap(jnp.where(even, top, bottom), "row", 1)
    near_rows = swap(jnp.where(even, bottom, top), "row", 0)
    own, wq, wkv_self, wkv_mutual, proj = call(
        own_kernel,
        [(2, 2, TOK, LANES), (LANES, 2 * LANES), (LANES, 2 * LANES), (LANES, 2 * LANES), (C, 2 * LANES)],
        (features, self_qkv, mutual_qkv, out_proj),
        name="own_kernel",
    )
    (block,) = call(
        halo_kernel, [(2, 4, TOK, LANES)], (far_rows, near_rows, own), name="halo_kernel"
    )
    far = swap(block, "tm", 1)
    near = swap(block, "tm", 0)
    nw = 2 * GROUPS
    queries, keys = (nw, 2 * PART, LANES), (nw, 4 * PART, LANES)
    self_out, qm = call(
        self_kernel,
        [(2, 2, TOK, LANES), queries],
        (block, wq, wkv_self),
        scratch=[queries, keys, keys],
        cost=2 * 10**9,
        name="self_attention",
    )
    knear, vnear = call(near_kernel, [keys, keys], (near, wkv_mutual), name="near_kernel")
    (result,) = call(
        mutual_kernel,
        [features.shape],
        (far, wkv_mutual, knear, vnear, qm, self_out, features, proj),
        scratch=[keys, keys, (2, 2, TOK, LANES)],
        cost=4 * 10**9,
        name="mutual_attention",
    )
    return result


def solution(mesh):
    in_specs = (P("tm", None, "row"), P(), P(), P())
    out_specs = P("tm", None, "row")
    return jax.shard_map(
        on_device, mesh=mesh, in_specs=in_specs, out_specs=out_specs, check_vma=False
    )
```

```python
import jax
import jax.numpy as jnp
from jax import lax
from jax.experimental import pallas as pl
from jax.experimental.pallas import tpu as pltpu
from jax.sharding import PartitionSpec as P

C = 120
HEADS = 6
HD = 20
WIN = 8
COLS = 32
HALF = WIN // 2
TOK = HALF * COLS
GROUPS = COLS // WIN
PART = HALF * WIN
LANES = 128
NEG = -1e30
F32 = jnp.float32
BF16 = jnp.bfloat16

NN = (((1,), (0,)), ((), ()))
NT = (((1,), (1,)), ((), ()))


def iota(shape, dim):
    return lax.broadcasted_iota(jnp.int32, shape, dim)


def dot(a, b, dims=NN):
    return lax.dot_general(a, b, dims, preferred_element_type=F32)


def window_order(transposed=False):
    tok, pos = (1, 0) if transposed else (0, 1)
    t = iota((TOK, TOK), tok)
    p = iota((TOK, TOK), pos)
    column = ((t // PART) * WIN + t % WIN + HALF) % COLS
    row = (t % PART) // WIN
    return jnp.where(row * COLS + column == p, 1.0, 0.0).astype(BF16)


def normalize(x, invalid):
    x = x.astype(F32)
    mean = jnp.mean(x, axis=0, keepdims=True)
    centered = x - mean
    spread = jnp.mean(centered * centered, axis=0, keepdims=True)
    normed = centered * lax.rsqrt(spread + 1e-05)
    sub = iota((LANES - C, x.shape[1]), 0)
    extra = jnp.where(sub == 0, invalid, jnp.where(sub == 1, 1.0, 0.0))
    return jnp.concatenate([normed, extra], axis=0).astype(BF16)


def padded(weights, part, at=None, value=0.0):
    w = weights[:, part * C : (part + 1) * C].astype(F32)
    w = jnp.concatenate([w, jnp.zeros((C, LANES - C), F32)], axis=1)
    w = jnp.concatenate([w, jnp.zeros((LANES - C, LANES), F32)], axis=0)
    if at is not None:
        hit = (iota((LANES, LANES), 0) == at) & (iota((LANES, LANES), 1) == C)
        w = jnp.where(hit, value, w)
    return w.astype(BF16)


def query_weights(weights):
    return padded(weights, 0, C + 1, 1.0)


def kv_weights(weights):
    return jnp.concatenate([padded(weights, 1, C, NEG), padded(weights, 2)], axis=1)


def score(q, k):
    lane = iota((1, LANES), 1)
    head_of = lane // HD
    zero = jnp.zeros_like(q)
    spread = [
        jnp.where((head_of == h) & (lane < C) | (lane == C), q, zero) for h in range(HEADS)
    ]
    return dot(jnp.concatenate(spread, axis=0), k, NT)


def softmax(scores):
    weights = jnp.exp(scores - jnp.max(scores, axis=-1, keepdims=True))
    return (weights * (1.0 / jnp.sum(weights, axis=-1, keepdims=True))).astype(BF16)


def pick_heads(out):
    lane = iota((1, LANES), 1)
    n = out.shape[0] // HEADS
    total = jnp.zeros((n, LANES), F32)
    for h in range(HEADS):
        total = jnp.where((lane // HD == h) & (lane < C), out[h * n : (h + 1) * n], total)
    return total.astype(BF16)


def attend(query, key, value, out_ref):
    count = 2 * GROUPS
    scores = [score(query(w), key(w)) for w in range(count)]
    weights = [softmax(x) for x in scores]
    for w in range(count):
        out = pick_heads(dot(weights[w], value(w)))
        for f in range(2):
            rows = slice((w % GROUPS) * PART, (w % GROUPS + 1) * PART)
            out_ref[f, w // GROUPS, rows, :] = out[f * PART : (f + 1) * PART]


def tokens(pair, order):
    out = dot(order, jnp.concatenate(pair, axis=0), NT).astype(BF16)
    return out[:, :LANES], out[:, LANES:]


def own_kernel(
    features_ref, self_ref, mutual_ref, proj_ref,
    tok_ref, wq_ref, wkv_self_ref, wkv_mutual_ref, proj_out_ref,
):
    order = window_order()
    for s in range(2):
        cut = slice(s * TOK, (s + 1) * TOK)
        pair = [normalize(features_ref[f, :, cut], 0.0) for f in range(2)]
        for f, tok in enumerate(tokens(pair, order)):
            tok_ref[f, s] = tok
    wq_ref[...] = jnp.concatenate([query_weights(self_ref), query_weights(mutual_ref)], axis=1)
    wkv_self_ref[...] = kv_weights(self_ref)
    wkv_mutual_ref[...] = kv_weights(mutual_ref)
    proj = proj_ref[...].astype(F32)
    gap = jnp.zeros((LANES - C, C), F32)
    proj = jnp.concatenate([proj[:C], gap, proj[C:], gap], axis=0)
    proj_out_ref[...] = proj.T.astype(BF16)


def halo_kernel(near_ref, far_ref, own_ref, block_ref):
    order = window_order()
    row = lax.axis_index("row")
    even = lax.rem(row, 2) == 0
    top = jnp.where(row == 0, 1.0, 0.0)
    bottom = jnp.where(row == lax.axis_size("row") - 1, 1.0, 0.0)
    for s, invalid in ((0, top), (3, bottom)):
        pair = []
        for f in range(2):
            far, near = far_ref[f].astype(F32), near_ref[f].astype(F32)
            pair.append(normalize(jnp.where(even == (s == 0), far, near), invalid))
        for f, tok in enumerate(tokens(pair, order)):
            block_ref[f, s] = tok
    for f in range(2):
        for s in range(2):
            block_ref[f, s + 1] = own_ref[f, s]


def store_keys(k_ref, v_ref, tokens, weights):
    kv = dot(tokens.reshape(8 * TOK, LANES), weights).astype(BF16)
    for f in range(2):
        for s in range(4):
            for n in range(GROUPS):
                start = (f * 4 + s) * TOK + n * PART
                w = (s // 2) * GROUPS + n
                slot = (s % 2) * 2 + f
                rows = slice(slot * PART, (slot + 1) * PART)
                k_ref[w, rows, :] = kv[start : start + PART, :LANES]
                v_ref[w, rows, :] = kv[start : start + PART, LANES:]


def self_kernel(block_ref, wq_ref, wkv_ref, out_ref, qm_ref, q_ref, k_ref, v_ref):
    own = jnp.concatenate([block_ref[f, s] for f in range(2) for s in (1, 2)], axis=0)
    queries = (dot(own, wq_ref[...]) * HD ** (-0.5)).astype(BF16)
    store_keys(k_ref, v_ref, block_ref[...], wkv_ref[...])
    for f in range(2):
        for w in range(2 * GROUPS):
            part = queries[(f * 2 * GROUPS + w) * PART : (f * 2 * GROUPS + w + 1) * PART]
            q_ref[w, f * PART : (f + 1) * PART, :] = part[:, :LANES]
            qm_ref[w, f * PART : (f + 1) * PART, :] = part[:, LANES:]
    attend(lambda w: q_ref[w], lambda w: k_ref[w], lambda w: v_ref[w], out_ref)


def mutual_kernel(
    near_ref, far_ref, wkv_ref, qm_ref, self_out_ref, features_ref, proj_ref,
    result_ref, knear_ref, vnear_ref, k_ref, v_ref, attn_ref,
):
    clip = lax.axis_index("tm")
    edge = (clip == 0) | (clip == lax.axis_size("tm") - 1)
    flag = jnp.where((iota((1, 1, 1, LANES), 3) == C) & edge, 1.0, 0.0).astype(BF16)
    store_keys(knear_ref, vnear_ref, near_ref[...], wkv_ref[...])
    store_keys(k_ref, v_ref, far_ref[...] + flag, wkv_ref[...])
    attend(
        lambda w: qm_ref[w],
        lambda w: jnp.concatenate([knear_ref[w], k_ref[w]], axis=0),
        lambda w: jnp.concatenate([vnear_ref[w], v_ref[w]], axis=0),
        attn_ref,
    )
    places = [(f, g) for f in range(2) for g in range(2)]
    mixed = [ref[f, g] for f, g in places for ref in (attn_ref, self_out_ref)]
    mixed = dot(window_order(transposed=True), jnp.concatenate(mixed, axis=1)).astype(BF16)
    wide = 2 * LANES
    mixed = jnp.concatenate([mixed[:, i * wide : (i + 1) * wide] for i in range(4)], axis=0)
    branch = dot(proj_ref[...], mixed, NT)
    for i, (f, g) in enumerate(places):
        cut = slice(g * TOK, (g + 1) * TOK)
        part = branch[:, i * TOK : (i + 1) * TOK]
        result_ref[f, :, cut] = (features_ref[f, :, cut].astype(F32) + part).astype(BF16)


def call(kernel, outs, args, scratch=(), cost=10**9, name=None):
    return pl.pallas_call(
        kernel,
        out_shape=[jax.ShapeDtypeStruct(shape, BF16) for shape in outs],
        in_specs=[pl.BlockSpec(memory_space=pltpu.VMEM)] * len(args),
        out_specs=[pl.BlockSpec(memory_space=pltpu.VMEM)] * len(outs),
        scratch_shapes=[pltpu.VMEM(shape, BF16) for shape in scratch],
        compiler_params=pltpu.CompilerParams(vmem_limit_bytes=16 * 1024 * 1024),
        cost_estimate=pl.CostEstimate(flops=cost, bytes_accessed=10**6, transcendentals=0),
        name=name,
    )(*args)


def swap(x, axis, first):
    pairs = [(i, i + 1) for i in range(first, lax.axis_size(axis) - 1, 2)]
    return lax.ppermute(x, axis, pairs + [(j, i) for i, j in pairs])


def on_device(features, self_qkv, mutual_qkv, out_proj):
    even = lax.axis_index("row") % 2 == 0
    top, bottom = features[:, :, :TOK], features[:, :, TOK:]
    far_rows = swap(jnp.where(even, top, bottom), "row", 1)
    near_rows = swap(jnp.where(even, bottom, top), "row", 0)
    own, wq, wkv_self, wkv_mutual, proj = call(
        own_kernel,
        [(2, 2, TOK, LANES), (LANES, 2 * LANES), (LANES, 2 * LANES), (LANES, 2 * LANES), (C, 2 * LANES)],
        (features, self_qkv, mutual_qkv, out_proj),
        name="own_kernel",
    )
    (block,) = call(
        halo_kernel, [(2, 4, TOK, LANES)], (near_rows, far_rows, own), name="halo_kernel"
    )
    far = swap(block, "tm", 1)
    near = swap(block, "tm", 0)
    nw = 2 * GROUPS
    queries, keys = (nw, 2 * PART, LANES), (nw, 4 * PART, LANES)
    self_out, qm = call(
        self_kernel,
        [(2, 2, TOK, LANES), queries],
        (block, wq, wkv_self),
        scratch=[queries, keys, keys],
        cost=2 * 10**9,
        name="self_attention",
    )
    (result,) = call(
        mutual_kernel,
        [features.shape],
        (near, far, wkv_mutual, qm, self_out, features, proj),
        scratch=[keys, keys, keys, keys, (2, 2, TOK, LANES)],
        cost=4 * 10**9,
        name="mutual_attention",
    )
    return result


def solution(mesh):
    in_specs = (P("tm", None, "row"), P(), P(), P())
    out_specs = P("tm", None, "row")
    return jax.shard_map(
        on_device, mesh=mesh, in_specs=in_specs, out_specs=out_specs, check_vma=False
    )
```

```python
import jax
import jax.numpy as jnp
from jax import lax
from jax.experimental import pallas as pl
from jax.experimental.pallas import tpu as pltpu
from jax.sharding import PartitionSpec as P

C = 120
HEADS = 6
HD = 20
WIN = 8
COLS = 32
HALF = WIN // 2
TOK = HALF * COLS
GROUPS = COLS // WIN
PART = HALF * WIN
LANES = 128
NEG = -1e30
F32 = jnp.float32
BF16 = jnp.bfloat16

NN = (((1,), (0,)), ((), ()))
NT = (((1,), (1,)), ((), ()))


def iota(shape, dim):
    return lax.broadcasted_iota(jnp.int32, shape, dim)


def dot(a, b, dims=NN):
    return lax.dot_general(a, b, dims, preferred_element_type=F32)


def window_order(transposed=False):
    tok, pos = (1, 0) if transposed else (0, 1)
    t = iota((TOK, TOK), tok)
    p = iota((TOK, TOK), pos)
    column = ((t // PART) * WIN + t % WIN + HALF) % COLS
    row = (t % PART) // WIN
    return jnp.where(row * COLS + column == p, 1.0, 0.0).astype(BF16)


def normalize(x, invalid):
    x = x.astype(F32)
    mean = jnp.mean(x, axis=0, keepdims=True)
    centered = x - mean
    spread = jnp.mean(centered * centered, axis=0, keepdims=True)
    normed = centered * lax.rsqrt(spread + 1e-05)
    sub = iota((LANES - C, x.shape[1]), 0)
    extra = jnp.where(sub == 0, invalid, jnp.where(sub == 1, 1.0, 0.0))
    return jnp.concatenate([normed, extra], axis=0).astype(BF16)


def padded(weights, part, at=None, value=0.0):
    w = weights[:, part * C : (part + 1) * C].astype(F32)
    w = jnp.concatenate([w, jnp.zeros((C, LANES - C), F32)], axis=1)
    w = jnp.concatenate([w, jnp.zeros((LANES - C, LANES), F32)], axis=0)
    if at is not None:
        hit = (iota((LANES, LANES), 0) == at) & (iota((LANES, LANES), 1) == C)
        w = jnp.where(hit, value, w)
    return w.astype(BF16)


def query_weights(weights):
    return padded(weights, 0, C + 1, 1.0)


def kv_weights(weights):
    return jnp.concatenate([padded(weights, 1, C, NEG), padded(weights, 2)], axis=1)


def score(q, k):
    lane = iota((1, LANES), 1)
    head_of = lane // HD
    zero = jnp.zeros_like(q)
    spread = [
        jnp.where((head_of == h) & (lane < C) | (lane == C), q, zero) for h in range(HEADS)
    ]
    return dot(jnp.concatenate(spread, axis=0), k, NT)


def softmax(scores):
    weights = jnp.exp(scores - jnp.max(scores, axis=-1, keepdims=True))
    return (weights * (1.0 / jnp.sum(weights, axis=-1, keepdims=True))).astype(BF16)


def pick_heads(out):
    lane = iota((1, LANES), 1)
    n = out.shape[0] // HEADS
    total = jnp.zeros((n, LANES), F32)
    for h in range(HEADS):
        total = jnp.where((lane // HD == h) & (lane < C), out[h * n : (h + 1) * n], total)
    return total.astype(BF16)


def attend(query, key, value, out_ref):
    count = 2 * GROUPS
    scores = [score(query(w), key(w)) for w in range(count)]
    weights = [softmax(x) for x in scores]
    for w in range(count):
        out = pick_heads(dot(weights[w], value(w)))
        for f in range(2):
            rows = slice((w % GROUPS) * PART, (w % GROUPS + 1) * PART)
            out_ref[f, w // GROUPS, rows, :] = out[f * PART : (f + 1) * PART]


def tokens(pair, order):
    out = dot(order, jnp.concatenate(pair, axis=0), NT).astype(BF16)
    return out[:, :LANES], out[:, LANES:]


def own_kernel(features_ref, tok_ref):
    order = window_order()
    for s in range(2):
        cut = slice(s * TOK, (s + 1) * TOK)
        pair = [normalize(features_ref[f, :, cut], 0.0) for f in range(2)]
        for f, tok in enumerate(tokens(pair, order)):
            tok_ref[f, s] = tok


def weights_kernel(
    self_ref, mutual_ref, proj_ref, wq_ref, wkv_self_ref, wkv_mutual_ref, proj_out_ref
):
    wq_ref[...] = jnp.concatenate([query_weights(self_ref), query_weights(mutual_ref)], axis=1)
    wkv_self_ref[...] = kv_weights(self_ref)
    wkv_mutual_ref[...] = kv_weights(mutual_ref)
    proj = proj_ref[...].astype(F32)
    gap = jnp.zeros((LANES - C, C), F32)
    proj = jnp.concatenate([proj[:C], gap, proj[C:], gap], axis=0)
    proj_out_ref[...] = proj.T.astype(BF16)


def halo_kernel(near_ref, far_ref, own_ref, wq_ref, block_ref, halo_ref):
    order = window_order()
    row = lax.axis_index("row")
    even = lax.rem(row, 2) == 0
    top = jnp.where(row == 0, 1.0, 0.0)
    bottom = jnp.where(row == lax.axis_size("row") - 1, 1.0, 0.0)
    for s, invalid in ((0, top), (3, bottom)):
        pair = []
        for f in range(2):
            far, near = far_ref[f].astype(F32), near_ref[f].astype(F32)
            pair.append(normalize(jnp.where(even == (s == 0), far, near), invalid))
        for f, tok in enumerate(tokens(pair, order)):
            block_ref[f, s] = tok
            halo_ref[f, s // 3] = tok
    for f in range(2):
        for s in range(2):
            block_ref[f, s + 1] = own_ref[f, s]


def store_keys(k_ref, v_ref, tokens, weights):
    kv = dot(jnp.concatenate(tokens, axis=0), weights).astype(BF16)
    for f in range(2):
        for s in range(4):
            for n in range(GROUPS):
                start = (f * 4 + s) * TOK + n * PART
                w = (s // 2) * GROUPS + n
                slot = (s % 2) * 2 + f
                rows = slice(slot * PART, (slot + 1) * PART)
                k_ref[w, rows, :] = kv[start : start + PART, :LANES]
                v_ref[w, rows, :] = kv[start : start + PART, LANES:]


def self_kernel(block_ref, wq_ref, wkv_ref, far_own_ref, out_ref, qm_ref, q_ref, k_ref, v_ref):
    own = jnp.concatenate([block_ref[f, s] for f in range(2) for s in (1, 2)], axis=0)
    queries = (dot(own, wq_ref[...]) * HD ** (-0.5)).astype(BF16)
    blocks = [block_ref[f, s] for f in range(2) for s in range(4)]
    store_keys(k_ref, v_ref, blocks, wkv_ref[...])
    for f in range(2):
        for w in range(2 * GROUPS):
            part = queries[(f * 2 * GROUPS + w) * PART : (f * 2 * GROUPS + w + 1) * PART]
            q_ref[w, f * PART : (f + 1) * PART, :] = part[:, :LANES]
            qm_ref[w, f * PART : (f + 1) * PART, :] = part[:, LANES:]
    attend(lambda w: q_ref[w], lambda w: k_ref[w], lambda w: v_ref[w], out_ref)


def far_kernel(halo_ref, own_ref, wkv_ref, k_ref, v_ref):
    clip = lax.axis_index("tm")
    edge = (clip == 0) | (clip == lax.axis_size("tm") - 1)
    flag = jnp.where((iota((1, LANES), 1) == C) & edge, 1.0, 0.0).astype(BF16)
    blocks = []
    for f in range(2):
        strips = (halo_ref[f, 0], own_ref[f, 0], own_ref[f, 1], halo_ref[f, 1])
        blocks += [strip + flag for strip in strips]
    store_keys(k_ref, v_ref, blocks, wkv_ref[...])


def mutual_kernel(
    near_ref, kfar_ref, vfar_ref, wkv_ref, qm_ref, self_out_ref, features_ref, proj_ref,
    result_ref, k_ref, v_ref, attn_ref,
):
    blocks = [near_ref[f, s] for f in range(2) for s in range(4)]
    store_keys(k_ref, v_ref, blocks, wkv_ref[...])
    attend(
        lambda w: qm_ref[w],
        lambda w: jnp.concatenate([kfar_ref[w], k_ref[w]], axis=0),
        lambda w: jnp.concatenate([vfar_ref[w], v_ref[w]], axis=0),
        attn_ref,
    )
    places = [(f, g) for f in range(2) for g in range(2)]
    mixed = [ref[f, g] for f, g in places for ref in (attn_ref, self_out_ref)]
    mixed = dot(window_order(transposed=True), jnp.concatenate(mixed, axis=1)).astype(BF16)
    wide = 2 * LANES
    mixed = jnp.concatenate([mixed[:, i * wide : (i + 1) * wide] for i in range(4)], axis=0)
    branch = dot(proj_ref[...], mixed, NT)
    for i, (f, g) in enumerate(places):
        cut = slice(g * TOK, (g + 1) * TOK)
        part = branch[:, i * TOK : (i + 1) * TOK]
        result_ref[f, :, cut] = (features_ref[f, :, cut].astype(F32) + part).astype(BF16)


def call(kernel, outs, args, scratch=(), cost=10**9, name=None):
    return pl.pallas_call(
        kernel,
        out_shape=[jax.ShapeDtypeStruct(shape, BF16) for shape in outs],
        in_specs=[pl.BlockSpec(memory_space=pltpu.VMEM)] * len(args),
        out_specs=[pl.BlockSpec(memory_space=pltpu.VMEM)] * len(outs),
        scratch_shapes=[pltpu.VMEM(shape, BF16) for shape in scratch],
        compiler_params=pltpu.CompilerParams(vmem_limit_bytes=16 * 1024 * 1024),
        cost_estimate=pl.CostEstimate(flops=cost, bytes_accessed=10**6, transcendentals=0),
        name=name,
    )(*args)


def swap(x, axis, first):
    pairs = [(i, i + 1) for i in range(first, lax.axis_size(axis) - 1, 2)]
    return lax.ppermute(x, axis, pairs + [(j, i) for i, j in pairs])


def on_device(features, self_qkv, mutual_qkv, out_proj):
    even = lax.axis_index("row") % 2 == 0
    top, bottom = features[:, :, :TOK], features[:, :, TOK:]
    far_rows = swap(jnp.where(even, top, bottom), "row", 1)
    near_rows = swap(jnp.where(even, bottom, top), "row", 0)
    strips, wide = (2, 2, TOK, LANES), (LANES, 2 * LANES)
    (own,) = call(own_kernel, [strips], (features,), name="own_kernel")
    far_own = swap(own, "tm", 1)
    wq, wkv_self, wkv_mutual, proj = call(
        weights_kernel,
        [wide, wide, wide, (C, 2 * LANES)],
        (self_qkv, mutual_qkv, out_proj),
        name="weights_kernel",
    )
    block, halo = call(
        halo_kernel,
        [(2, 4, TOK, LANES), strips],
        (near_rows, far_rows, own, wq),
        name="halo_kernel",
    )
    far_halo = swap(halo, "tm", 1)
    near = swap(block, "tm", 0)
    nw = 2 * GROUPS
    queries, keys = (nw, 2 * PART, LANES), (nw, 4 * PART, LANES)
    self_out, qm = call(
        self_kernel,
        [strips, queries],
        (block, wq, wkv_self, far_own),
        scratch=[queries, keys, keys],
        cost=2 * 10**9,
        name="self_attention",
    )
    kfar, vfar = call(
        far_kernel,
        [keys, keys],
        (far_halo, far_own, wkv_mutual),
        cost=10**10,
        name="far_kernel",
    )
    (result,) = call(
        mutual_kernel,
        [features.shape],
        (near, kfar, vfar, wkv_mutual, qm, self_out, features, proj),
        scratch=[keys, keys, strips],
        cost=4 * 10**9,
        name="mutual_attention",
    )
    return result


def solution(mesh):
    in_specs = (P("tm", None, "row"), P(), P(), P())
    out_specs = P("tm", None, "row")
    return jax.shard_map(
        on_device, mesh=mesh, in_specs=in_specs, out_specs=out_specs, check_vma=False
    )
```

```python
import jax
import jax.numpy as jnp
from jax import lax
from jax.experimental import pallas as pl
from jax.experimental.pallas import tpu as pltpu
from jax.sharding import PartitionSpec as P

C = 120
HEADS = 6
HD = 20
WIN = 8
COLS = 32
HALF = WIN // 2
TOK = HALF * COLS
GROUPS = COLS // WIN
PART = HALF * WIN
LANES = 128
NEG = -1e30
F32 = jnp.float32
BF16 = jnp.bfloat16

NN = (((1,), (0,)), ((), ()))
NT = (((1,), (1,)), ((), ()))


def iota(shape, dim):
    return lax.broadcasted_iota(jnp.int32, shape, dim)


def dot(a, b, dims=NN):
    return lax.dot_general(a, b, dims, preferred_element_type=F32)


def window_order(transposed=False):
    tok, pos = (1, 0) if transposed else (0, 1)
    t = iota((TOK, TOK), tok)
    p = iota((TOK, TOK), pos)
    column = ((t // PART) * WIN + t % WIN + HALF) % COLS
    row = (t % PART) // WIN
    return jnp.where(row * COLS + column == p, 1.0, 0.0).astype(BF16)


def normalize(x, invalid):
    x = x.astype(F32)
    mean = jnp.mean(x, axis=0, keepdims=True)
    centered = x - mean
    spread = jnp.mean(centered * centered, axis=0, keepdims=True)
    normed = centered * lax.rsqrt(spread + 1e-05)
    sub = iota((LANES - C, x.shape[1]), 0)
    extra = jnp.where(sub == 0, invalid, jnp.where(sub == 1, 1.0, 0.0))
    return jnp.concatenate([normed, extra], axis=0).astype(BF16)


def padded(weights, part, at=None, value=0.0):
    w = weights[:, part * C : (part + 1) * C].astype(F32)
    w = jnp.concatenate([w, jnp.zeros((C, LANES - C), F32)], axis=1)
    w = jnp.concatenate([w, jnp.zeros((LANES - C, LANES), F32)], axis=0)
    if at is not None:
        hit = (iota((LANES, LANES), 0) == at) & (iota((LANES, LANES), 1) == C)
        w = jnp.where(hit, value, w)
    return w.astype(BF16)


def query_weights(weights):
    return padded(weights, 0, C + 1, 1.0)


def kv_weights(weights):
    return jnp.concatenate([padded(weights, 1, C, NEG), padded(weights, 2)], axis=1)


def score(q, k):
    lane = iota((1, LANES), 1)
    head_of = lane // HD
    zero = jnp.zeros_like(q)
    spread = [
        jnp.where((head_of == h) & (lane < C) | (lane == C), q, zero) for h in range(HEADS)
    ]
    return dot(jnp.concatenate(spread, axis=0), k, NT)


def softmax(scores):
    weights = jnp.exp(scores - jnp.max(scores, axis=-1, keepdims=True))
    return (weights * (1.0 / jnp.sum(weights, axis=-1, keepdims=True))).astype(BF16)


def pick_heads(out):
    lane = iota((1, LANES), 1)
    n = out.shape[0] // HEADS
    total = jnp.zeros((n, LANES), F32)
    for h in range(HEADS):
        total = jnp.where((lane // HD == h) & (lane < C), out[h * n : (h + 1) * n], total)
    return total.astype(BF16)


def attend(query, key, value, out_ref):
    count = 2 * GROUPS
    scores = [score(query(w), key(w)) for w in range(count)]
    weights = [softmax(x) for x in scores]
    for w in range(count):
        out = pick_heads(dot(weights[w], value(w)))
        for f in range(2):
            rows = slice((w % GROUPS) * PART, (w % GROUPS + 1) * PART)
            out_ref[f, w // GROUPS, rows, :] = out[f * PART : (f + 1) * PART]


def tokens(pair, order):
    out = dot(order, jnp.concatenate(pair, axis=0), NT).astype(BF16)
    return out[:, :LANES], out[:, LANES:]


def own_kernel(features_ref, tok_ref):
    order = window_order()
    for s in range(2):
        cut = slice(s * TOK, (s + 1) * TOK)
        pair = [normalize(features_ref[f, :, cut], 0.0) for f in range(2)]
        for f, tok in enumerate(tokens(pair, order)):
            tok_ref[f, s] = tok


def weights_kernel(
    self_ref, mutual_ref, proj_ref, halo_ref,
    wq_ref, wkv_self_ref, wkv_mutual_ref, proj_out_ref,
):
    wq_ref[...] = jnp.concatenate([query_weights(self_ref), query_weights(mutual_ref)], axis=1)
    wkv_self_ref[...] = kv_weights(self_ref)
    wkv_mutual_ref[...] = kv_weights(mutual_ref)
    proj = proj_ref[...].astype(F32)
    gap = jnp.zeros((LANES - C, C), F32)
    proj = jnp.concatenate([proj[:C], gap, proj[C:], gap], axis=0)
    proj_out_ref[...] = proj.T.astype(BF16)


def halo_kernel(far_ref, near_ref, own_ref, block_ref, halo_ref):
    order = window_order()
    row = lax.axis_index("row")
    even = lax.rem(row, 2) == 0
    top = jnp.where(row == 0, 1.0, 0.0)
    bottom = jnp.where(row == lax.axis_size("row") - 1, 1.0, 0.0)
    for s, invalid in ((0, top), (3, bottom)):
        pair = []
        for f in range(2):
            far, near = far_ref[f].astype(F32), near_ref[f].astype(F32)
            pair.append(normalize(jnp.where(even == (s == 0), far, near), invalid))
        for f, tok in enumerate(tokens(pair, order)):
            block_ref[f, s] = tok
            halo_ref[f, s // 3] = tok
    for f in range(2):
        for s in range(2):
            block_ref[f, s + 1] = own_ref[f, s]


def store_keys(k_ref, v_ref, tokens, weights):
    kv = dot(jnp.concatenate(tokens, axis=0), weights).astype(BF16)
    for f in range(2):
        for s in range(4):
            for n in range(GROUPS):
                start = (f * 4 + s) * TOK + n * PART
                w = (s // 2) * GROUPS + n
                slot = (s % 2) * 2 + f
                rows = slice(slot * PART, (slot + 1) * PART)
                k_ref[w, rows, :] = kv[start : start + PART, :LANES]
                v_ref[w, rows, :] = kv[start : start + PART, LANES:]


def self_kernel(block_ref, wq_ref, wkv_ref, far_own_ref, out_ref, qm_ref, q_ref, k_ref, v_ref):
    own = jnp.concatenate([block_ref[f, s] for f in range(2) for s in (1, 2)], axis=0)
    queries = (dot(own, wq_ref[...]) * HD ** (-0.5)).astype(BF16)
    blocks = [block_ref[f, s] for f in range(2) for s in range(4)]
    store_keys(k_ref, v_ref, blocks, wkv_ref[...])
    for f in range(2):
        for w in range(2 * GROUPS):
            part = queries[(f * 2 * GROUPS + w) * PART : (f * 2 * GROUPS + w + 1) * PART]
            q_ref[w, f * PART : (f + 1) * PART, :] = part[:, :LANES]
            qm_ref[w, f * PART : (f + 1) * PART, :] = part[:, LANES:]
    attend(lambda w: q_ref[w], lambda w: k_ref[w], lambda w: v_ref[w], out_ref)


def far_kernel(halo_ref, own_ref, wkv_ref, k_ref, v_ref):
    clip = lax.axis_index("tm")
    edge = (clip == 0) | (clip == lax.axis_size("tm") - 1)
    flag = jnp.where((iota((1, LANES), 1) == C) & edge, 1.0, 0.0).astype(BF16)
    blocks = []
    for f in range(2):
        strips = (halo_ref[f, 0], own_ref[f, 0], own_ref[f, 1], halo_ref[f, 1])
        blocks += [strip + flag for strip in strips]
    store_keys(k_ref, v_ref, blocks, wkv_ref[...])


def mutual_kernel(
    near_ref, kfar_ref, vfar_ref, wkv_ref, qm_ref, self_out_ref, features_ref, proj_ref,
    result_ref, k_ref, v_ref, attn_ref,
):
    blocks = [near_ref[f, s] for f in range(2) for s in range(4)]
    store_keys(k_ref, v_ref, blocks, wkv_ref[...])
    attend(
        lambda w: qm_ref[w],
        lambda w: jnp.concatenate([kfar_ref[w], k_ref[w]], axis=0),
        lambda w: jnp.concatenate([vfar_ref[w], v_ref[w]], axis=0),
        attn_ref,
    )
    places = [(f, g) for f in range(2) for g in range(2)]
    mixed = [ref[f, g] for f, g in places for ref in (attn_ref, self_out_ref)]
    mixed = dot(window_order(transposed=True), jnp.concatenate(mixed, axis=1)).astype(BF16)
    wide = 2 * LANES
    mixed = jnp.concatenate([mixed[:, i * wide : (i + 1) * wide] for i in range(4)], axis=0)
    branch = dot(proj_ref[...], mixed, NT)
    for i, (f, g) in enumerate(places):
        cut = slice(g * TOK, (g + 1) * TOK)
        part = branch[:, i * TOK : (i + 1) * TOK]
        result_ref[f, :, cut] = (features_ref[f, :, cut].astype(F32) + part).astype(BF16)


def call(kernel, outs, args, scratch=(), cost=10**9, name=None):
    return pl.pallas_call(
        kernel,
        out_shape=[jax.ShapeDtypeStruct(shape, BF16) for shape in outs],
        in_specs=[pl.BlockSpec(memory_space=pltpu.VMEM)] * len(args),
        out_specs=[pl.BlockSpec(memory_space=pltpu.VMEM)] * len(outs),
        scratch_shapes=[pltpu.VMEM(shape, BF16) for shape in scratch],
        compiler_params=pltpu.CompilerParams(vmem_limit_bytes=16 * 1024 * 1024),
        cost_estimate=pl.CostEstimate(flops=cost, bytes_accessed=10**6, transcendentals=0),
        name=name,
    )(*args)


def swap(x, axis, first):
    pairs = [(i, i + 1) for i in range(first, lax.axis_size(axis) - 1, 2)]
    return lax.ppermute(x, axis, pairs + [(j, i) for i, j in pairs])


def on_device(features, self_qkv, mutual_qkv, out_proj):
    even = lax.axis_index("row") % 2 == 0
    top, bottom = features[:, :, :TOK], features[:, :, TOK:]
    far_rows = swap(jnp.where(even, top, bottom), "row", 1)
    near_rows = swap(jnp.where(even, bottom, top), "row", 0)
    strips, wide = (2, 2, TOK, LANES), (LANES, 2 * LANES)
    (own,) = call(own_kernel, [strips], (features,), name="own_kernel")
    far_own = swap(own, "tm", 1)
    block, halo = call(
        halo_kernel,
        [(2, 4, TOK, LANES), strips],
        (far_rows, near_rows, own),
        name="halo_kernel",
    )
    wq, wkv_self, wkv_mutual, proj = call(
        weights_kernel,
        [wide, wide, wide, (C, 2 * LANES)],
        (self_qkv, mutual_qkv, out_proj, halo),
        name="weights_kernel",
    )
    far_halo = swap(halo, "tm", 1)
    near = swap(block, "tm", 0)
    nw = 2 * GROUPS
    queries, keys = (nw, 2 * PART, LANES), (nw, 4 * PART, LANES)
    self_out, qm = call(
        self_kernel,
        [strips, queries],
        (block, wq, wkv_self, far_own),
        scratch=[queries, keys, keys],
        cost=2 * 10**9,
        name="self_attention",
    )
    kfar, vfar = call(
        far_kernel,
        [keys, keys],
        (far_halo, far_own, wkv_mutual),
        cost=10**10,
        name="far_kernel",
    )
    (result,) = call(
        mutual_kernel,
        [features.shape],
        (near, kfar, vfar, wkv_mutual, qm, self_out, features, proj),
        scratch=[keys, keys, strips],
        cost=4 * 10**9,
        name="mutual_attention",
    )
    return result


def solution(mesh):
    in_specs = (P("tm", None, "row"), P(), P(), P())
    out_specs = P("tm", None, "row")
    return jax.shard_map(
        on_device, mesh=mesh, in_specs=in_specs, out_specs=out_specs, check_vma=False
    )
```

```python
import jax
import jax.numpy as jnp
from jax import lax
from jax.experimental import pallas as pl
from jax.experimental.pallas import tpu as pltpu
from jax.sharding import PartitionSpec as P

C = 120
HEADS = 6
HD = 20
WIN = 8
COLS = 32
HALF = WIN // 2
TOK = HALF * COLS
GROUPS = COLS // WIN
PART = HALF * WIN
LANES = 128
NEG = -1e30
F32 = jnp.float32
BF16 = jnp.bfloat16

NN = (((1,), (0,)), ((), ()))
NT = (((1,), (1,)), ((), ()))


def iota(shape, dim):
    return lax.broadcasted_iota(jnp.int32, shape, dim)


def dot(a, b, dims=NN):
    return lax.dot_general(a, b, dims, preferred_element_type=F32)


def window_order(transposed=False):
    tok, pos = (1, 0) if transposed else (0, 1)
    t = iota((TOK, TOK), tok)
    p = iota((TOK, TOK), pos)
    column = ((t // PART) * WIN + t % WIN + HALF) % COLS
    row = (t % PART) // WIN
    return jnp.where(row * COLS + column == p, 1.0, 0.0).astype(BF16)


def normalize(x, invalid):
    x = x.astype(F32)
    mean = jnp.mean(x, axis=0, keepdims=True)
    centered = x - mean
    spread = jnp.mean(centered * centered, axis=0, keepdims=True)
    normed = centered * lax.rsqrt(spread + 1e-05)
    sub = iota((LANES - C, x.shape[1]), 0)
    extra = jnp.where(sub == 0, invalid, jnp.where(sub == 1, 1.0, 0.0))
    return jnp.concatenate([normed, extra], axis=0).astype(BF16)


def padded(weights, part, at=None, value=0.0):
    w = weights[:, part * C : (part + 1) * C].astype(F32)
    w = jnp.concatenate([w, jnp.zeros((C, LANES - C), F32)], axis=1)
    w = jnp.concatenate([w, jnp.zeros((LANES - C, LANES), F32)], axis=0)
    if at is not None:
        hit = (iota((LANES, LANES), 0) == at) & (iota((LANES, LANES), 1) == C)
        w = jnp.where(hit, value, w)
    return w.astype(BF16)


def query_weights(weights):
    return padded(weights, 0, C + 1, 1.0)


def kv_weights(weights):
    return jnp.concatenate([padded(weights, 1, C, NEG), padded(weights, 2)], axis=1)


def score(q, k):
    lane = iota((1, LANES), 1)
    head_of = lane // HD
    zero = jnp.zeros_like(q)
    spread = [
        jnp.where((head_of == h) & (lane < C) | (lane == C), q, zero) for h in range(HEADS)
    ]
    return dot(jnp.concatenate(spread, axis=0), k, NT)


def softmax(scores):
    weights = jnp.exp(scores - jnp.max(scores, axis=-1, keepdims=True))
    return (weights * (1.0 / jnp.sum(weights, axis=-1, keepdims=True))).astype(BF16)


def pick_heads(out):
    lane = iota((1, LANES), 1)
    n = out.shape[0] // HEADS
    total = jnp.zeros((n, LANES), F32)
    for h in range(HEADS):
        total = jnp.where((lane // HD == h) & (lane < C), out[h * n : (h + 1) * n], total)
    return total.astype(BF16)


def attend(query, key, value, out_ref):
    count = 2 * GROUPS
    scores = [score(query(w), key(w)) for w in range(count)]
    weights = [softmax(x) for x in scores]
    for w in range(count):
        out = pick_heads(dot(weights[w], value(w)))
        for f in range(2):
            rows = slice((w % GROUPS) * PART, (w % GROUPS + 1) * PART)
            out_ref[f, w // GROUPS, rows, :] = out[f * PART : (f + 1) * PART]


def tokens(pair, order):
    out = dot(order, jnp.concatenate(pair, axis=0), NT).astype(BF16)
    return out[:, :LANES], out[:, LANES:]


def own_kernel(features_ref, tok_ref):
    order = window_order()
    for s in range(2):
        cut = slice(s * TOK, (s + 1) * TOK)
        pair = [normalize(features_ref[f, :, cut], 0.0) for f in range(2)]
        for f, tok in enumerate(tokens(pair, order)):
            tok_ref[f, s] = tok


def weights_kernel(
    self_ref, mutual_ref, proj_ref, halo_ref,
    wq_ref, wkv_self_ref, wkv_mutual_ref, proj_out_ref,
):
    wq_ref[...] = jnp.concatenate([query_weights(self_ref), query_weights(mutual_ref)], axis=1)
    wkv_self_ref[...] = kv_weights(self_ref)
    wkv_mutual_ref[...] = kv_weights(mutual_ref)
    proj = proj_ref[...].astype(F32)
    gap = jnp.zeros((LANES - C, C), F32)
    proj = jnp.concatenate([proj[:C], gap, proj[C:], gap], axis=0)
    proj_out_ref[...] = proj.T.astype(BF16)


def halo_kernel(far_ref, near_ref, own_ref, block_ref, halo_ref):
    order = window_order()
    row = lax.axis_index("row")
    even = lax.rem(row, 2) == 0
    top = jnp.where(row == 0, 1.0, 0.0)
    bottom = jnp.where(row == lax.axis_size("row") - 1, 1.0, 0.0)
    for s, invalid in ((0, top), (3, bottom)):
        pair = []
        for f in range(2):
            far, near = far_ref[f].astype(F32), near_ref[f].astype(F32)
            pair.append(normalize(jnp.where(even == (s == 0), far, near), invalid))
        for f, tok in enumerate(tokens(pair, order)):
            block_ref[f, s] = tok
            halo_ref[f, s // 3] = tok
    for f in range(2):
        for s in range(2):
            block_ref[f, s + 1] = own_ref[f, s]


def store_keys(k_ref, v_ref, strips, weights):
    kv = dot(jnp.concatenate([tok for tok, _, _ in strips], axis=0), weights).astype(BF16)
    for i, (_, g, slot) in enumerate(strips):
        rows = slice(slot * PART, (slot + 1) * PART)
        for n in range(GROUPS):
            start = i * TOK + n * PART
            k_ref[g * GROUPS + n, rows, :] = kv[start : start + PART, :LANES]
            v_ref[g * GROUPS + n, rows, :] = kv[start : start + PART, LANES:]


def block_strips(get):
    return [(get(f, s), s // 2, (s % 2) * 2 + f) for f in range(2) for s in range(4)]


def edge_flag():
    clip = lax.axis_index("tm")
    edge = (clip == 0) | (clip == lax.axis_size("tm") - 1)
    return jnp.where((iota((1, LANES), 1) == C) & edge, 1.0, 0.0).astype(BF16)


def self_kernel(block_ref, wq_ref, wkv_ref, far_own_ref, out_ref, qm_ref, q_ref, k_ref, v_ref):
    own = jnp.concatenate([block_ref[f, s] for f in range(2) for s in (1, 2)], axis=0)
    queries = (dot(own, wq_ref[...]) * HD ** (-0.5)).astype(BF16)
    store_keys(k_ref, v_ref, block_strips(lambda f, s: block_ref[f, s]), wkv_ref[...])
    for f in range(2):
        for w in range(2 * GROUPS):
            part = queries[(f * 2 * GROUPS + w) * PART : (f * 2 * GROUPS + w + 1) * PART]
            q_ref[w, f * PART : (f + 1) * PART, :] = part[:, :LANES]
            qm_ref[w, f * PART : (f + 1) * PART, :] = part[:, LANES:]
    attend(lambda w: q_ref[w], lambda w: k_ref[w], lambda w: v_ref[w], out_ref)


def early_kernel(near_ref, own_ref, wkv_ref, k_ref, v_ref):
    other = 1 - lax.rem(lax.axis_index("tm"), 2)
    flag = edge_flag()
    strips = block_strips(lambda f, s: near_ref[other, f, s])
    strips += [(own_ref[f, g] + flag, g, 4 + f) for f in range(2) for g in range(2)]
    store_keys(k_ref, v_ref, strips, wkv_ref[...])


def mutual_kernel(
    halo_ref, kearly_ref, vearly_ref, wkv_ref, qm_ref, self_out_ref, features_ref, proj_ref,
    result_ref, k_ref, v_ref, attn_ref,
):
    flag = edge_flag()
    strips = [(halo_ref[f, g] + flag, g, f) for f in range(2) for g in range(2)]
    store_keys(k_ref, v_ref, strips, wkv_ref[...])
    attend(
        lambda w: qm_ref[w],
        lambda w: jnp.concatenate([kearly_ref[w], k_ref[w]], axis=0),
        lambda w: jnp.concatenate([vearly_ref[w], v_ref[w]], axis=0),
        attn_ref,
    )
    places = [(f, g) for f in range(2) for g in range(2)]
    mixed = [ref[f, g] for f, g in places for ref in (attn_ref, self_out_ref)]
    mixed = dot(window_order(transposed=True), jnp.concatenate(mixed, axis=1)).astype(BF16)
    wide = 2 * LANES
    mixed = jnp.concatenate([mixed[:, i * wide : (i + 1) * wide] for i in range(4)], axis=0)
    branch = dot(proj_ref[...], mixed, NT)
    for i, (f, g) in enumerate(places):
        cut = slice(g * TOK, (g + 1) * TOK)
        part = branch[:, i * TOK : (i + 1) * TOK]
        result_ref[f, :, cut] = (features_ref[f, :, cut].astype(F32) + part).astype(BF16)


def call(kernel, outs, args, scratch=(), cost=10**9, name=None):
    return pl.pallas_call(
        kernel,
        out_shape=[jax.ShapeDtypeStruct(shape, BF16) for shape in outs],
        in_specs=[pl.BlockSpec(memory_space=pltpu.VMEM)] * len(args),
        out_specs=[pl.BlockSpec(memory_space=pltpu.VMEM)] * len(outs),
        scratch_shapes=[pltpu.VMEM(shape, BF16) for shape in scratch],
        compiler_params=pltpu.CompilerParams(vmem_limit_bytes=16 * 1024 * 1024),
        cost_estimate=pl.CostEstimate(flops=cost, bytes_accessed=10**6, transcendentals=0),
        name=name,
    )(*args)


def swap(x, axis, first):
    pairs = [(i, i + 1) for i in range(first, lax.axis_size(axis) - 1, 2)]
    return lax.ppermute(x, axis, pairs + [(j, i) for i, j in pairs])


def on_device(features, self_qkv, mutual_qkv, out_proj):
    even = lax.axis_index("row") % 2 == 0
    top, bottom = features[:, :, :TOK], features[:, :, TOK:]
    far_rows = swap(jnp.where(even, top, bottom), "row", 1)
    near_rows = swap(jnp.where(even, bottom, top), "row", 0)
    strips, wide = (2, 2, TOK, LANES), (LANES, 2 * LANES)
    (own,) = call(own_kernel, [strips], (features,), name="own_kernel")
    far_own = swap(own, "tm", 1)
    block, halo = call(
        halo_kernel,
        [(2, 4, TOK, LANES), strips],
        (far_rows, near_rows, own),
        name="halo_kernel",
    )
    wq, wkv_self, wkv_mutual, proj = call(
        weights_kernel,
        [wide, wide, wide, (C, 2 * LANES)],
        (self_qkv, mutual_qkv, out_proj, halo),
        cost=10**6,
        name="weights_kernel",
    )
    far_halo = swap(halo, "tm", 1)
    chips = [[i, i + 1] for i in range(0, lax.axis_size("tm"), 2)]
    near = lax.all_gather(block, "tm", axis_index_groups=chips)
    nw = 2 * GROUPS
    queries, keys = (nw, 2 * PART, LANES), (nw, 4 * PART, LANES)
    self_out, qm = call(
        self_kernel,
        [strips, queries],
        (block, wq, wkv_self, far_own),
        scratch=[queries, keys, keys],
        cost=10**6,
        name="self_attention",
    )
    early, late = (nw, 6 * PART, LANES), (nw, 2 * PART, LANES)
    kearly, vearly = call(
        early_kernel, [early, early], (near, far_own, wkv_mutual), cost=10**6, name="early_kernel"
    )
    (result,) = call(
        mutual_kernel,
        [features.shape],
        (far_halo, kearly, vearly, wkv_mutual, qm, self_out, features, proj),
        scratch=[late, late, strips],
        cost=4 * 10**9,
        name="mutual_attention",
    )
    return result


def solution(mesh):
    in_specs = (P("tm", None, "row"), P(), P(), P())
    out_specs = P("tm", None, "row")
    return jax.shard_map(
        on_device, mesh=mesh, in_specs=in_specs, out_specs=out_specs, check_vma=False
    )
```

```python
import jax
import jax.numpy as jnp
from jax import lax
from jax.experimental import pallas as pl
from jax.experimental.pallas import tpu as pltpu
from jax.sharding import PartitionSpec as P

C = 120
HEADS = 6
HD = 20
WIN = 8
COLS = 32
HALF = WIN // 2
TOK = HALF * COLS
GROUPS = COLS // WIN
PART = HALF * WIN
LANES = 128
NEG = -1e30
F32 = jnp.float32
BF16 = jnp.bfloat16

NN = (((1,), (0,)), ((), ()))
NT = (((1,), (1,)), ((), ()))


def iota(shape, dim):
    return lax.broadcasted_iota(jnp.int32, shape, dim)


def dot(a, b, dims=NN):
    return lax.dot_general(a, b, dims, preferred_element_type=F32)


def window_order(transposed=False):
    tok, pos = (1, 0) if transposed else (0, 1)
    t = iota((TOK, TOK), tok)
    p = iota((TOK, TOK), pos)
    column = ((t // PART) * WIN + t % WIN + HALF) % COLS
    row = (t % PART) // WIN
    return jnp.where(row * COLS + column == p, 1.0, 0.0).astype(BF16)


def normalize(x, invalid):
    x = x.astype(F32)
    mean = jnp.mean(x, axis=0, keepdims=True)
    centered = x - mean
    spread = jnp.mean(centered * centered, axis=0, keepdims=True)
    normed = centered * lax.rsqrt(spread + 1e-05)
    sub = iota((LANES - C, x.shape[1]), 0)
    extra = jnp.where(sub == 0, invalid, jnp.where(sub == 1, 1.0, 0.0))
    return jnp.concatenate([normed, extra], axis=0).astype(BF16)


def padded(weights, part, at=None, value=0.0):
    w = weights[:, part * C : (part + 1) * C].astype(F32)
    w = jnp.concatenate([w, jnp.zeros((C, LANES - C), F32)], axis=1)
    w = jnp.concatenate([w, jnp.zeros((LANES - C, LANES), F32)], axis=0)
    if at is not None:
        hit = (iota((LANES, LANES), 0) == at) & (iota((LANES, LANES), 1) == C)
        w = jnp.where(hit, value, w)
    return w.astype(BF16)


def query_weights(weights):
    return padded(weights, 0, C + 1, 1.0)


def kv_weights(weights):
    return jnp.concatenate([padded(weights, 1, C, NEG), padded(weights, 2)], axis=1)


def score(q, k):
    lane = iota((1, LANES), 1)
    head_of = lane // HD
    zero = jnp.zeros_like(q)
    spread = [
        jnp.where((head_of == h) & (lane < C) | (lane == C), q, zero) for h in range(HEADS)
    ]
    return dot(jnp.concatenate(spread, axis=0), k, NT)


def softmax(scores):
    weights = jnp.exp(scores - jnp.max(scores, axis=-1, keepdims=True))
    return (weights * (1.0 / jnp.sum(weights, axis=-1, keepdims=True))).astype(BF16)


def pick_heads(out):
    lane = iota((1, LANES), 1)
    n = out.shape[0] // HEADS
    total = jnp.zeros((n, LANES), F32)
    for h in range(HEADS):
        total = jnp.where((lane // HD == h) & (lane < C), out[h * n : (h + 1) * n], total)
    return total.astype(BF16)


def attend(query, key, value, out_ref):
    count = 2 * GROUPS
    scores = [score(query(w), key(w)) for w in range(count)]
    weights = [softmax(x) for x in scores]
    for w in range(count):
        out = pick_heads(dot(weights[w], value(w)))
        for f in range(2):
            rows = slice((w % GROUPS) * PART, (w % GROUPS + 1) * PART)
            out_ref[f, w // GROUPS, rows, :] = out[f * PART : (f + 1) * PART]


def tokens(pair, order):
    out = dot(order, jnp.concatenate(pair, axis=0), NT).astype(BF16)
    return out[:, :LANES], out[:, LANES:]


def order_kernel(order_ref):
    order_ref[...] = window_order()


def own_kernel(features_ref, order_ref, tok_ref, copy_ref):
    copy_ref[...] = features_ref[...]
    order = order_ref[...]
    for s in range(2):
        cut = slice(s * TOK, (s + 1) * TOK)
        pair = [normalize(features_ref[f, :, cut], 0.0) for f in range(2)]
        for f, tok in enumerate(tokens(pair, order)):
            tok_ref[f, s] = tok


def weights_kernel(
    self_ref, mutual_ref, proj_ref, halo_ref, wq_ref, wkv_self_ref, wkv_mutual_ref, proj_out_ref,
):
    wq_ref[...] = jnp.concatenate([query_weights(self_ref), query_weights(mutual_ref)], axis=1)
    wkv_self_ref[...] = kv_weights(self_ref)
    wkv_mutual_ref[...] = kv_weights(mutual_ref)
    proj = proj_ref[...].astype(F32)
    gap = jnp.zeros((LANES - C, C), F32)
    proj = jnp.concatenate([proj[:C], gap, proj[C:], gap], axis=0)
    proj_out_ref[...] = proj.T.astype(BF16)


def halo_kernel(far_ref, near_ref, own_ref, order_ref, block_ref, halo_ref):
    order = order_ref[...]
    row = lax.axis_index("row")
    even = lax.rem(row, 2) == 0
    top = jnp.where(row == 0, 1.0, 0.0)
    bottom = jnp.where(row == lax.axis_size("row") - 1, 1.0, 0.0)
    for s, invalid in ((0, top), (3, bottom)):
        pair = []
        for f in range(2):
            cut = slice(TOK, 2 * TOK) if s == 0 else slice(0, TOK)
            far, near = far_ref[f, :, cut].astype(F32), near_ref[f, :, cut].astype(F32)
            pair.append(normalize(jnp.where(even == (s == 0), far, near), invalid))
        for f, tok in enumerate(tokens(pair, order)):
            block_ref[f, s] = tok
            halo_ref[f, s // 3] = tok
    for f in range(2):
        for s in range(2):
            block_ref[f, s + 1] = own_ref[f, s]


def store_keys(k_ref, v_ref, strips, weights):
    kv = dot(jnp.concatenate([tok for tok, _, _ in strips], axis=0), weights).astype(BF16)
    for i, (_, g, slot) in enumerate(strips):
        rows = slice(slot * PART, (slot + 1) * PART)
        for n in range(GROUPS):
            start = i * TOK + n * PART
            k_ref[g * GROUPS + n, rows, :] = kv[start : start + PART, :LANES]
            v_ref[g * GROUPS + n, rows, :] = kv[start : start + PART, LANES:]


def block_strips(get):
    return [(get(f, s), s // 2, (s % 2) * 2 + f) for f in range(2) for s in range(4)]


def edge_flag():
    clip = lax.axis_index("tm")
    edge = (clip == 0) | (clip == lax.axis_size("tm") - 1)
    return jnp.where((iota((1, LANES), 1) == C) & edge, 1.0, 0.0).astype(BF16)


def self_kernel(block_ref, wq_ref, wkv_ref, far_own_ref, out_ref, qm_ref, q_ref, k_ref, v_ref):
    own = jnp.concatenate([block_ref[f, s] for f in range(2) for s in (1, 2)], axis=0)
    queries = (dot(own, wq_ref[...]) * HD ** (-0.5)).astype(BF16)
    store_keys(k_ref, v_ref, block_strips(lambda f, s: block_ref[f, s]), wkv_ref[...])
    for f in range(2):
        for w in range(2 * GROUPS):
            part = queries[(f * 2 * GROUPS + w) * PART : (f * 2 * GROUPS + w + 1) * PART]
            q_ref[w, f * PART : (f + 1) * PART, :] = part[:, :LANES]
            qm_ref[w, f * PART : (f + 1) * PART, :] = part[:, LANES:]
    attend(lambda w: q_ref[w], lambda w: k_ref[w], lambda w: v_ref[w], out_ref)


def early_kernel(near_ref, far_ref, wkv_ref, k_ref, v_ref):
    other = 1 - lax.rem(lax.axis_index("tm"), 2)
    clip = lax.axis_index("tm")
    edge = (clip == 0) | (clip == lax.axis_size("tm") - 1)
    strips = block_strips(lambda f, s: near_ref[other, f, s])
    order = window_order()
    for g in range(2):
        cut = slice(g * TOK, (g + 1) * TOK)
        pair = [normalize(far_ref[f, :, cut], jnp.where(edge, 1.0, 0.0)) for f in range(2)]
        strips += [(tok, g, 4 + f) for f, tok in enumerate(tokens(pair, order))]
    store_keys(k_ref, v_ref, strips, wkv_ref[...])


def mutual_kernel(
    halo_ref, kearly_ref, vearly_ref, wkv_ref, qm_ref, self_out_ref, features_ref, proj_ref,
    result_ref, k_ref, v_ref, attn_ref,
):
    flag = edge_flag()
    strips = [(halo_ref[f, g] + flag, g, f) for f in range(2) for g in range(2)]
    store_keys(k_ref, v_ref, strips, wkv_ref[...])
    attend(
        lambda w: qm_ref[w],
        lambda w: jnp.concatenate([kearly_ref[w], k_ref[w]], axis=0),
        lambda w: jnp.concatenate([vearly_ref[w], v_ref[w]], axis=0),
        attn_ref,
    )
    places = [(f, g) for f in range(2) for g in range(2)]
    mixed = [ref[f, g] for f, g in places for ref in (attn_ref, self_out_ref)]
    mixed = dot(window_order(transposed=True), jnp.concatenate(mixed, axis=1)).astype(BF16)
    wide = 2 * LANES
    mixed = jnp.concatenate([mixed[:, i * wide : (i + 1) * wide] for i in range(4)], axis=0)
    branch = dot(proj_ref[...], mixed, NT)
    for i, (f, g) in enumerate(places):
        cut = slice(g * TOK, (g + 1) * TOK)
        part = branch[:, i * TOK : (i + 1) * TOK]
        result_ref[f, :, cut] = (features_ref[f, :, cut].astype(F32) + part).astype(BF16)


def call(kernel, outs, args, scratch=(), cost=10**9, name=None):
    return pl.pallas_call(
        kernel,
        out_shape=[jax.ShapeDtypeStruct(shape, BF16) for shape in outs],
        in_specs=[pl.BlockSpec(memory_space=pltpu.VMEM)] * len(args),
        out_specs=[pl.BlockSpec(memory_space=pltpu.VMEM)] * len(outs),
        scratch_shapes=[pltpu.VMEM(shape, BF16) for shape in scratch],
        compiler_params=pltpu.CompilerParams(vmem_limit_bytes=16 * 1024 * 1024),
        cost_estimate=pl.CostEstimate(flops=cost, bytes_accessed=10**6, transcendentals=0),
        name=name,
    )(*args)


def swap(x, axis, first):
    pairs = [(i, i + 1) for i in range(first, lax.axis_size(axis) - 1, 2)]
    return lax.ppermute(x, axis, pairs + [(j, i) for i, j in pairs])


def on_device(features, self_qkv, mutual_qkv, out_proj):
    near_rows = swap(features, "row", 0)
    strips, wide = (2, 2, TOK, LANES), (LANES, 2 * LANES)
    far_rows = swap(features, "row", 1)
    far_own = swap(features, "tm", 1)
    (order,) = call(order_kernel, [(TOK, TOK)], (), name="order_kernel")
    own, kept = call(own_kernel, [strips, features.shape], (features, order), name="own_kernel")
    block, halo = call(
        halo_kernel,
        [(2, 4, TOK, LANES), strips],
        (far_rows, near_rows, own, order),
        name="halo_kernel",
    )
    wq, wkv_self, wkv_mutual, proj = call(
        weights_kernel,
        [wide, wide, wide, (C, 2 * LANES)],
        (self_qkv, mutual_qkv, out_proj, halo),
        cost=10**6,
        name="weights_kernel",
    )
    far_halo = swap(halo, "tm", 1)
    chips = [[i, i + 1] for i in range(0, lax.axis_size("tm"), 2)]
    near = lax.all_gather(block, "tm", axis_index_groups=chips)
    nw = 2 * GROUPS
    queries, keys = (nw, 2 * PART, LANES), (nw, 4 * PART, LANES)
    self_out, qm = call(
        self_kernel,
        [strips, queries],
        (block, wq, wkv_self, far_own),
        scratch=[queries, keys, keys],
        cost=10**6,
        name="self_attention",
    )
    early, late = (nw, 6 * PART, LANES), (nw, 2 * PART, LANES)
    kearly, vearly = call(
        early_kernel, [early, early], (near, far_own, wkv_mutual), cost=10**6, name="early_kernel"
    )
    (result,) = call(
        mutual_kernel,
        [features.shape],
        (far_halo, kearly, vearly, wkv_mutual, qm, self_out, kept, proj),
        scratch=[late, late, strips],
        cost=4 * 10**9,
        name="mutual_attention",
    )
    return result


def solution(mesh):
    in_specs = (P("tm", None, "row"), P(), P(), P())
    out_specs = P("tm", None, "row")
    return jax.shard_map(
        on_device, mesh=mesh, in_specs=in_specs, out_specs=out_specs, check_vma=False
    )
```

```python
import jax
import jax.numpy as jnp
from jax import lax
from jax.experimental import pallas as pl
from jax.experimental.pallas import tpu as pltpu
from jax.sharding import PartitionSpec as P

C = 120
HEADS = 6
HD = 20
WIN = 8
COLS = 32
HALF = WIN // 2
TOK = HALF * COLS
GROUPS = COLS // WIN
PART = HALF * WIN
LANES = 128
NEG = -1e30
F32 = jnp.float32
BF16 = jnp.bfloat16

NN = (((1,), (0,)), ((), ()))
NT = (((1,), (1,)), ((), ()))


def iota(shape, dim):
    return lax.broadcasted_iota(jnp.int32, shape, dim)


def dot(a, b, dims=NN):
    return lax.dot_general(a, b, dims, preferred_element_type=F32)


def window_order(transposed=False):
    tok, pos = (1, 0) if transposed else (0, 1)
    t = iota((TOK, TOK), tok)
    p = iota((TOK, TOK), pos)
    column = ((t // PART) * WIN + t % WIN + HALF) % COLS
    row = (t % PART) // WIN
    return jnp.where(row * COLS + column == p, 1.0, 0.0).astype(BF16)


def normalize(x, invalid):
    x = x.astype(F32)
    mean = jnp.mean(x, axis=0, keepdims=True)
    centered = x - mean
    spread = jnp.mean(centered * centered, axis=0, keepdims=True)
    normed = centered * lax.rsqrt(spread + 1e-05)
    sub = iota((LANES - C, x.shape[1]), 0)
    extra = jnp.where(sub == 0, invalid, jnp.where(sub == 1, 1.0, 0.0))
    return jnp.concatenate([normed, extra], axis=0).astype(BF16)


def padded(weights, part, at=None, value=0.0):
    w = weights[:, part * C : (part + 1) * C].astype(F32)
    w = jnp.concatenate([w, jnp.zeros((C, LANES - C), F32)], axis=1)
    w = jnp.concatenate([w, jnp.zeros((LANES - C, LANES), F32)], axis=0)
    if at is not None:
        hit = (iota((LANES, LANES), 0) == at) & (iota((LANES, LANES), 1) == C)
        w = jnp.where(hit, value, w)
    return w.astype(BF16)


def query_weights(weights):
    return padded(weights, 0, C + 1, 1.0)


def kv_weights(weights):
    return jnp.concatenate([padded(weights, 1, C, NEG), padded(weights, 2)], axis=1)


def score(q, k):
    lane = iota((1, LANES), 1)
    head_of = lane // HD
    zero = jnp.zeros_like(q)
    spread = [
        jnp.where((head_of == h) & (lane < C) | (lane == C), q, zero) for h in range(HEADS)
    ]
    return dot(jnp.concatenate(spread, axis=0), k, NT)


def softmax(scores):
    weights = jnp.exp(scores - jnp.max(scores, axis=-1, keepdims=True))
    return (weights * (1.0 / jnp.sum(weights, axis=-1, keepdims=True))).astype(BF16)


def pick_heads(out):
    lane = iota((1, LANES), 1)
    n = out.shape[0] // HEADS
    total = jnp.zeros((n, LANES), F32)
    for h in range(HEADS):
        total = jnp.where((lane // HD == h) & (lane < C), out[h * n : (h + 1) * n], total)
    return total.astype(BF16)


def attend(query, key, value, out_ref):
    count = 2 * GROUPS
    scores = [score(query(w), key(w)) for w in range(count)]
    weights = [softmax(x) for x in scores]
    for w in range(count):
        out = pick_heads(dot(weights[w], value(w)))
        for f in range(2):
            rows = slice((w % GROUPS) * PART, (w % GROUPS + 1) * PART)
            out_ref[f, w // GROUPS, rows, :] = out[f * PART : (f + 1) * PART]


def tokens(pair, order):
    out = dot(order, jnp.concatenate(pair, axis=0), NT).astype(BF16)
    return out[:, :LANES], out[:, LANES:]


def order_kernel(order_ref):
    order_ref[...] = window_order()


def own_kernel(features_ref, order_ref, tok_ref, copy_ref):
    copy_ref[...] = features_ref[...]
    order = order_ref[...]
    for s in range(2):
        cut = slice(s * TOK, (s + 1) * TOK)
        pair = [normalize(features_ref[f, :, cut], 0.0) for f in range(2)]
        for f, tok in enumerate(tokens(pair, order)):
            tok_ref[f, s] = tok


def weights_kernel(
    self_ref, mutual_ref, proj_ref, halo_ref, wq_ref, wkv_self_ref, wkv_mutual_ref, proj_out_ref,
):
    wq_ref[...] = jnp.concatenate([query_weights(self_ref), query_weights(mutual_ref)], axis=1)
    wkv_self_ref[...] = kv_weights(self_ref)
    wkv_mutual_ref[...] = kv_weights(mutual_ref)
    proj = proj_ref[...].astype(F32)
    gap = jnp.zeros((LANES - C, C), F32)
    proj = jnp.concatenate([proj[:C], gap, proj[C:], gap], axis=0)
    proj_out_ref[...] = proj.T.astype(BF16)


def halo_kernel(far_ref, near_ref, own_ref, order_ref, block_ref, halo_ref):
    order = order_ref[...]
    row = lax.axis_index("row")
    even = lax.rem(row, 2) == 0
    top = jnp.where(row == 0, 1.0, 0.0)
    bottom = jnp.where(row == lax.axis_size("row") - 1, 1.0, 0.0)
    for s, invalid in ((0, top), (3, bottom)):
        pair = []
        for f in range(2):
            cut = slice(TOK, 2 * TOK) if s == 0 else slice(0, TOK)
            far, near = far_ref[f, :, cut].astype(F32), near_ref[f, :, cut].astype(F32)
            pair.append(normalize(jnp.where(even == (s == 0), far, near), invalid))
        for f, tok in enumerate(tokens(pair, order)):
            block_ref[f, s] = tok
            halo_ref[f, s // 3] = tok
    for f in range(2):
        for s in range(2):
            block_ref[f, s + 1] = own_ref[f, s]


def store_keys(k_ref, v_ref, strips, weights):
    kv = dot(jnp.concatenate([tok for tok, _, _ in strips], axis=0), weights).astype(BF16)
    for i, (_, g, slot) in enumerate(strips):
        rows = slice(slot * PART, (slot + 1) * PART)
        for n in range(GROUPS):
            start = i * TOK + n * PART
            k_ref[g * GROUPS + n, rows, :] = kv[start : start + PART, :LANES]
            v_ref[g * GROUPS + n, rows, :] = kv[start : start + PART, LANES:]


def block_strips(get):
    return [(get(f, s), s // 2, (s % 2) * 2 + f) for f in range(2) for s in range(4)]


def edge_flag():
    clip = lax.axis_index("tm")
    edge = (clip == 0) | (clip == lax.axis_size("tm") - 1)
    return jnp.where((iota((1, LANES), 1) == C) & edge, 1.0, 0.0).astype(BF16)


def self_kernel(
    block_ref, wq_ref, wkv_ref, far_ref, wkv_mutual_ref, order_ref, near_ref,
    out_ref, qm_ref, kearly_ref, vearly_ref, q_ref, k_ref, v_ref,
):
    clip = lax.axis_index("tm")
    edge = (clip == 0) | (clip == lax.axis_size("tm") - 1)
    other = 1 - lax.rem(clip, 2)
    strips = block_strips(lambda f, s: near_ref[other, f, s])
    for g in range(2):
        cut = slice(g * TOK, (g + 1) * TOK)
        pair = [normalize(far_ref[f, :, cut], jnp.where(edge, 1.0, 0.0)) for f in range(2)]
        strips += [(tok, g, 4 + f) for f, tok in enumerate(tokens(pair, order_ref[...]))]
    store_keys(kearly_ref, vearly_ref, strips, wkv_mutual_ref[...])
    own = jnp.concatenate([block_ref[f, s] for f in range(2) for s in (1, 2)], axis=0)
    queries = (dot(own, wq_ref[...]) * HD ** (-0.5)).astype(BF16)
    store_keys(k_ref, v_ref, block_strips(lambda f, s: block_ref[f, s]), wkv_ref[...])
    for f in range(2):
        for w in range(2 * GROUPS):
            part = queries[(f * 2 * GROUPS + w) * PART : (f * 2 * GROUPS + w + 1) * PART]
            q_ref[w, f * PART : (f + 1) * PART, :] = part[:, :LANES]
            qm_ref[w, f * PART : (f + 1) * PART, :] = part[:, LANES:]
    attend(lambda w: q_ref[w], lambda w: k_ref[w], lambda w: v_ref[w], out_ref)


def mutual_kernel(
    halo_ref, kearly_ref, vearly_ref, wkv_ref, qm_ref, self_out_ref, features_ref, proj_ref,
    result_ref, k_ref, v_ref, attn_ref,
):
    flag = edge_flag()
    strips = [(halo_ref[f, g] + flag, g, f) for f in range(2) for g in range(2)]
    store_keys(k_ref, v_ref, strips, wkv_ref[...])
    attend(
        lambda w: qm_ref[w],
        lambda w: jnp.concatenate([k_ref[w], kearly_ref[w]], axis=0),
        lambda w: jnp.concatenate([v_ref[w], vearly_ref[w]], axis=0),
        attn_ref,
    )
    places = [(f, g) for f in range(2) for g in range(2)]
    mixed = [ref[f, g] for f, g in places for ref in (attn_ref, self_out_ref)]
    mixed = dot(window_order(transposed=True), jnp.concatenate(mixed, axis=1)).astype(BF16)
    wide = 2 * LANES
    mixed = jnp.concatenate([mixed[:, i * wide : (i + 1) * wide] for i in range(4)], axis=0)
    branch = dot(proj_ref[...], mixed, NT)
    for i, (f, g) in enumerate(places):
        cut = slice(g * TOK, (g + 1) * TOK)
        part = branch[:, i * TOK : (i + 1) * TOK]
        result_ref[f, :, cut] = (features_ref[f, :, cut].astype(F32) + part).astype(BF16)


def call(kernel, outs, args, scratch=(), cost=10**9, name=None):
    return pl.pallas_call(
        kernel,
        out_shape=[jax.ShapeDtypeStruct(shape, BF16) for shape in outs],
        in_specs=[pl.BlockSpec(memory_space=pltpu.VMEM)] * len(args),
        out_specs=[pl.BlockSpec(memory_space=pltpu.VMEM)] * len(outs),
        scratch_shapes=[pltpu.VMEM(shape, BF16) for shape in scratch],
        compiler_params=pltpu.CompilerParams(vmem_limit_bytes=16 * 1024 * 1024),
        cost_estimate=pl.CostEstimate(flops=cost, bytes_accessed=10**6, transcendentals=0),
        name=name,
    )(*args)


def swap(x, axis, first):
    pairs = [(i, i + 1) for i in range(first, lax.axis_size(axis) - 1, 2)]
    return lax.ppermute(x, axis, pairs + [(j, i) for i, j in pairs])


def on_device(features, self_qkv, mutual_qkv, out_proj):
    near_rows = swap(features, "row", 0)
    strips, wide = (2, 2, TOK, LANES), (LANES, 2 * LANES)
    far_rows = swap(features, "row", 1)
    far_own = swap(features, "tm", 1)
    (order,) = call(order_kernel, [(TOK, TOK)], (), name="order_kernel")
    own, kept = call(own_kernel, [strips, features.shape], (features, order), name="own_kernel")
    block, halo = call(
        halo_kernel,
        [(2, 4, TOK, LANES), strips],
        (far_rows, near_rows, own, order),
        name="halo_kernel",
    )
    wq, wkv_self, wkv_mutual, proj = call(
        weights_kernel,
        [wide, wide, wide, (C, 2 * LANES)],
        (self_qkv, mutual_qkv, out_proj, halo),
        cost=10**6,
        name="weights_kernel",
    )
    far_halo = swap(halo, "tm", 1)
    chips = [[i, i + 1] for i in range(0, lax.axis_size("tm"), 2)]
    near = lax.all_gather(block, "tm", axis_index_groups=chips)
    nw = 2 * GROUPS
    queries, keys = (nw, 2 * PART, LANES), (nw, 4 * PART, LANES)
    early, late = (nw, 6 * PART, LANES), (nw, 2 * PART, LANES)
    self_out, qm, kearly, vearly = call(
        self_kernel,
        [strips, queries, early, early],
        (block, wq, wkv_self, far_own, wkv_mutual, order, near),
        scratch=[queries, keys, keys],
        cost=10**6,
        name="self_attention",
    )
    (result,) = call(
        mutual_kernel,
        [features.shape],
        (far_halo, kearly, vearly, wkv_mutual, qm, self_out, kept, proj),
        scratch=[late, late, strips],
        cost=4 * 10**9,
        name="mutual_attention",
    )
    return result


def solution(mesh):
    in_specs = (P("tm", None, "row"), P(), P(), P())
    out_specs = P("tm", None, "row")
    return jax.shard_map(
        on_device, mesh=mesh, in_specs=in_specs, out_specs=out_specs, check_vma=False
    )
```

```python
import jax
import jax.numpy as jnp
from jax import lax
from jax.experimental import pallas as pl
from jax.experimental.pallas import tpu as pltpu
from jax.sharding import PartitionSpec as P

C = 120
HEADS = 6
HD = 20
WIN = 8
COLS = 32
HALF = WIN // 2
TOK = HALF * COLS
GROUPS = COLS // WIN
PART = HALF * WIN
LANES = 128
NEG = -1e30
F32 = jnp.float32
BF16 = jnp.bfloat16

NN = (((1,), (0,)), ((), ()))
NT = (((1,), (1,)), ((), ()))


def iota(shape, dim):
    return lax.broadcasted_iota(jnp.int32, shape, dim)


def dot(a, b, dims=NN):
    return lax.dot_general(a, b, dims, preferred_element_type=F32)


def window_order(transposed=False):
    tok, pos = (1, 0) if transposed else (0, 1)
    t = iota((TOK, TOK), tok)
    p = iota((TOK, TOK), pos)
    column = ((t // PART) * WIN + t % WIN + HALF) % COLS
    row = (t % PART) // WIN
    return jnp.where(row * COLS + column == p, 1.0, 0.0).astype(BF16)


def normalize(x, invalid):
    x = x.astype(F32)
    mean = jnp.mean(x, axis=0, keepdims=True)
    centered = x - mean
    spread = jnp.mean(centered * centered, axis=0, keepdims=True)
    normed = centered * lax.rsqrt(spread + 1e-05)
    sub = iota((LANES - C, x.shape[1]), 0)
    extra = jnp.where(sub == 0, invalid, jnp.where(sub == 1, 1.0, 0.0))
    return jnp.concatenate([normed, extra], axis=0).astype(BF16)


def padded(weights, part, at=None, value=0.0):
    w = weights[:, part * C : (part + 1) * C].astype(F32)
    w = jnp.concatenate([w, jnp.zeros((C, LANES - C), F32)], axis=1)
    w = jnp.concatenate([w, jnp.zeros((LANES - C, LANES), F32)], axis=0)
    if at is not None:
        hit = (iota((LANES, LANES), 0) == at) & (iota((LANES, LANES), 1) == C)
        w = jnp.where(hit, value, w)
    return w.astype(BF16)


def query_weights(weights):
    return padded(weights, 0, C + 1, 1.0)


def kv_weights(weights):
    return jnp.concatenate([padded(weights, 1, C, NEG), padded(weights, 2)], axis=1)


def score(q, k):
    lane = iota((1, LANES), 1)
    head_of = lane // HD
    zero = jnp.zeros_like(q)
    spread = [
        jnp.where((head_of == h) & (lane < C) | (lane == C), q, zero) for h in range(HEADS)
    ]
    return dot(jnp.concatenate(spread, axis=0), k, NT)


def softmax(scores):
    weights = jnp.exp(scores - jnp.max(scores, axis=-1, keepdims=True))
    return (weights * pl.reciprocal(jnp.sum(weights, axis=-1, keepdims=True))).astype(BF16)


def pick_heads(out):
    lane = iota((1, LANES), 1)
    n = out.shape[0] // HEADS
    total = jnp.zeros((n, LANES), F32)
    for h in range(HEADS):
        total = jnp.where((lane // HD == h) & (lane < C), out[h * n : (h + 1) * n], total)
    return total.astype(BF16)


def attend(query, key, value, out_ref):
    count = 2 * GROUPS
    scores = [score(query(w), key(w)) for w in range(count)]
    weights = [softmax(x) for x in scores]
    for w in range(count):
        out = pick_heads(dot(weights[w], value(w)))
        for f in range(2):
            rows = slice((w % GROUPS) * PART, (w % GROUPS + 1) * PART)
            out_ref[f, w // GROUPS, rows, :] = out[f * PART : (f + 1) * PART]


def tokens(pair, order):
    out = dot(order, jnp.concatenate(pair, axis=0), NT).astype(BF16)
    return out[:, :LANES], out[:, LANES:]


def order_kernel(order_ref):
    order_ref[...] = window_order()


def own_kernel(features_ref, order_ref, tok_ref, copy_ref):
    copy_ref[...] = features_ref[...]
    order = order_ref[...]
    for s in range(2):
        cut = slice(s * TOK, (s + 1) * TOK)
        pair = [normalize(features_ref[f, :, cut], 0.0) for f in range(2)]
        for f, tok in enumerate(tokens(pair, order)):
            tok_ref[f, s] = tok


def weights_kernel(
    self_ref, mutual_ref, proj_ref, halo_ref, wq_ref, wkv_self_ref, wkv_mutual_ref, proj_out_ref,
):
    wq_ref[...] = jnp.concatenate([query_weights(self_ref), query_weights(mutual_ref)], axis=1)
    wkv_self_ref[...] = kv_weights(self_ref)
    wkv_mutual_ref[...] = kv_weights(mutual_ref)
    proj = proj_ref[...].astype(F32)
    gap = jnp.zeros((LANES - C, C), F32)
    proj = jnp.concatenate([proj[:C], gap, proj[C:], gap], axis=0)
    proj_out_ref[...] = proj.T.astype(BF16)


def halo_kernel(far_ref, near_ref, own_ref, order_ref, block_ref, halo_ref):
    order = order_ref[...]
    row = lax.axis_index("row")
    even = lax.rem(row, 2) == 0
    top = jnp.where(row == 0, 1.0, 0.0)
    bottom = jnp.where(row == lax.axis_size("row") - 1, 1.0, 0.0)
    for s, invalid in ((0, top), (3, bottom)):
        pair = []
        for f in range(2):
            cut = slice(TOK, 2 * TOK) if s == 0 else slice(0, TOK)
            far, near = far_ref[f, :, cut].astype(F32), near_ref[f, :, cut].astype(F32)
            pair.append(normalize(jnp.where(even == (s == 0), far, near), invalid))
        for f, tok in enumerate(tokens(pair, order)):
            block_ref[f, s] = tok
            halo_ref[f, s // 3] = tok
    for f in range(2):
        for s in range(2):
            block_ref[f, s + 1] = own_ref[f, s]


def store_keys(k_ref, v_ref, strips, weights):
    kv = dot(jnp.concatenate([tok for tok, _, _ in strips], axis=0), weights).astype(BF16)
    for i, (_, g, slot) in enumerate(strips):
        rows = slice(slot * PART, (slot + 1) * PART)
        for n in range(GROUPS):
            start = i * TOK + n * PART
            k_ref[g * GROUPS + n, rows, :] = kv[start : start + PART, :LANES]
            v_ref[g * GROUPS + n, rows, :] = kv[start : start + PART, LANES:]


def block_strips(get):
    return [(get(f, s), s // 2, (s % 2) * 2 + f) for f in range(2) for s in range(4)]


def edge_flag():
    clip = lax.axis_index("tm")
    edge = (clip == 0) | (clip == lax.axis_size("tm") - 1)
    return jnp.where((iota((1, LANES), 1) == C) & edge, 1.0, 0.0).astype(BF16)


def self_kernel(
    block_ref, wq_ref, wkv_ref, far_ref, wkv_mutual_ref, order_ref, near_ref,
    out_ref, qm_ref, kearly_ref, vearly_ref, q_ref, k_ref, v_ref,
):
    clip = lax.axis_index("tm")
    edge = (clip == 0) | (clip == lax.axis_size("tm") - 1)
    other = 1 - lax.rem(clip, 2)
    strips = block_strips(lambda f, s: near_ref[other, f, s])
    for g in range(2):
        cut = slice(g * TOK, (g + 1) * TOK)
        pair = [normalize(far_ref[f, :, cut], jnp.where(edge, 1.0, 0.0)) for f in range(2)]
        strips += [(tok, g, 4 + f) for f, tok in enumerate(tokens(pair, order_ref[...]))]
    store_keys(kearly_ref, vearly_ref, strips, wkv_mutual_ref[...])
    own = jnp.concatenate([block_ref[f, s] for f in range(2) for s in (1, 2)], axis=0)
    queries = (dot(own, wq_ref[...]) * HD ** (-0.5)).astype(BF16)
    store_keys(k_ref, v_ref, block_strips(lambda f, s: block_ref[f, s]), wkv_ref[...])
    for f in range(2):
        for w in range(2 * GROUPS):
            part = queries[(f * 2 * GROUPS + w) * PART : (f * 2 * GROUPS + w + 1) * PART]
            q_ref[w, f * PART : (f + 1) * PART, :] = part[:, :LANES]
            qm_ref[w, f * PART : (f + 1) * PART, :] = part[:, LANES:]
    attend(lambda w: q_ref[w], lambda w: k_ref[w], lambda w: v_ref[w], out_ref)


def mutual_kernel(
    halo_ref, kearly_ref, vearly_ref, wkv_ref, qm_ref, self_out_ref, features_ref, proj_ref,
    result_ref, k_ref, v_ref, attn_ref,
):
    flag = edge_flag()
    strips = [(halo_ref[f, g] + flag, g, f) for f in range(2) for g in range(2)]
    store_keys(k_ref, v_ref, strips, wkv_ref[...])
    attend(
        lambda w: qm_ref[w],
        lambda w: jnp.concatenate([k_ref[w], kearly_ref[w]], axis=0),
        lambda w: jnp.concatenate([v_ref[w], vearly_ref[w]], axis=0),
        attn_ref,
    )
    places = [(f, g) for f in range(2) for g in range(2)]
    mixed = [ref[f, g] for f, g in places for ref in (attn_ref, self_out_ref)]
    mixed = dot(window_order(transposed=True), jnp.concatenate(mixed, axis=1)).astype(BF16)
    wide = 2 * LANES
    mixed = jnp.concatenate([mixed[:, i * wide : (i + 1) * wide] for i in range(4)], axis=0)
    branch = dot(proj_ref[...], mixed, NT)
    for i, (f, g) in enumerate(places):
        cut = slice(g * TOK, (g + 1) * TOK)
        part = branch[:, i * TOK : (i + 1) * TOK]
        result_ref[f, :, cut] = (features_ref[f, :, cut].astype(F32) + part).astype(BF16)


def call(kernel, outs, args, scratch=(), cost=10**9, name=None):
    return pl.pallas_call(
        kernel,
        out_shape=[jax.ShapeDtypeStruct(shape, BF16) for shape in outs],
        in_specs=[pl.BlockSpec(memory_space=pltpu.VMEM)] * len(args),
        out_specs=[pl.BlockSpec(memory_space=pltpu.VMEM)] * len(outs),
        scratch_shapes=[pltpu.VMEM(shape, BF16) for shape in scratch],
        compiler_params=pltpu.CompilerParams(vmem_limit_bytes=16 * 1024 * 1024),
        cost_estimate=pl.CostEstimate(flops=cost, bytes_accessed=10**6, transcendentals=0),
        name=name,
    )(*args)


def swap(x, axis, first):
    pairs = [(i, i + 1) for i in range(first, lax.axis_size(axis) - 1, 2)]
    return lax.ppermute(x, axis, pairs + [(j, i) for i, j in pairs])


def on_device(features, self_qkv, mutual_qkv, out_proj):
    near_rows = swap(features, "row", 0)
    strips, wide = (2, 2, TOK, LANES), (LANES, 2 * LANES)
    far_rows = swap(features, "row", 1)
    far_own = swap(features, "tm", 1)
    (order,) = call(order_kernel, [(TOK, TOK)], (), name="order_kernel")
    own, kept = call(own_kernel, [strips, features.shape], (features, order), name="own_kernel")
    block, halo = call(
        halo_kernel,
        [(2, 4, TOK, LANES), strips],
        (far_rows, near_rows, own, order),
        name="halo_kernel",
    )
    wq, wkv_self, wkv_mutual, proj = call(
        weights_kernel,
        [wide, wide, wide, (C, 2 * LANES)],
        (self_qkv, mutual_qkv, out_proj, halo),
        cost=10**6,
        name="weights_kernel",
    )
    far_halo = swap(halo, "tm", 1)
    chips = [[i, i + 1] for i in range(0, lax.axis_size("tm"), 2)]
    near = lax.all_gather(block, "tm", axis_index_groups=chips)
    nw = 2 * GROUPS
    queries, keys = (nw, 2 * PART, LANES), (nw, 4 * PART, LANES)
    early, late = (nw, 6 * PART, LANES), (nw, 2 * PART, LANES)
    self_out, qm, kearly, vearly = call(
        self_kernel,
        [strips, queries, early, early],
        (block, wq, wkv_self, far_own, wkv_mutual, order, near),
        scratch=[queries, keys, keys],
        cost=10**6,
        name="self_attention",
    )
    (result,) = call(
        mutual_kernel,
        [features.shape],
        (far_halo, kearly, vearly, wkv_mutual, qm, self_out, kept, proj),
        scratch=[late, late, strips],
        cost=4 * 10**9,
        name="mutual_attention",
    )
    return result


def solution(mesh):
    in_specs = (P("tm", None, "row"), P(), P(), P())
    out_specs = P("tm", None, "row")
    return jax.shard_map(
        on_device, mesh=mesh, in_specs=in_specs, out_specs=out_specs, check_vma=False
    )
```
